128 devices in a mesh: expert: 32 (over z, y, core), group: 4 (over x).
Axes of the slice: x: 4, y: 4, z: 4, core: 2. Of those that a mesh axis runs over, the one named last changes fastest.
Arguments:
- tokens: bfloat16 [16384, 2048], P(('expert', 'group')), may hold values from -6 to 6
- low_tap: bfloat16 [16384, 2048], P(('expert', 'group')), may hold values from -6 to 6
- mid_tap: bfloat16 [16384, 2048], P(('expert', 'group')), may hold values from -6 to 6
- next_embed: bfloat16 [16384, 2048], P(('expert', 'group')), may hold values from -6 to 6
- expert_ids: int32 [16384, 8], P(('expert', 'group')), may hold values from 0 to 127, all different within a row; in each aligned block of 128 rows (0 to 127, 128 to 255, ...) at most 12 rows name the same one
- gate_weights: float32 [16384, 8], P(('expert', 'group')), may hold values from 0.02 to 0.3
- segments: int32 [16384], replicated, may hold values from 0 to 3, never falling along the last dimension, each value on 1 to 8192 neighbouring positions
- moe_gain: float32 [2048], replicated, may hold values from 0.1 to 1.9
- w_gate: bfloat16 [128, 2048, 768], P(('expert', 'group')), may hold values from -0.125 to 0.125
- w_up: bfloat16 [128, 2048, 768], P(('expert', 'group')), may hold values from -0.125 to 0.125
- w_down: bfloat16 [128, 768, 2048], P(('expert', 'group')), may hold values from -0.21875 to 0.21875
- merge_weight: bfloat16 [6144, 2048], P(None, 'group'), may hold values from -0.078125 to 0.078125
- embed_gain: float32 [2048], replicated, may hold values from 0.1 to 1.9
- merged_gain: float32 [2048], replicated, may hold values from 0.1 to 1.9
- w_query: bfloat16 [4096, 2048], P(None, 'group'), may hold values from -0.09375 to 0.09375
- w_kv: bfloat16 [4096, 2, 512], P(None, None, 'group'), may hold values from -0.09375 to 0.09375
- q_gain: float32 [128], replicated, may hold values from 2 to 3
- k_gain: float32 [128], replicated, may hold values from 2 to 3
Outputs:
- attended: bfloat16 [16384, 2048], P('expert', 'group')
The draws below stay inside these ranges and needn't reach their ends.
Inputs may be any that keep to these rules, and one draw needn't show every extreme that they name: `expert_ids`: each row names 8 different experts; within the rows of one device no expert is named by more than 12 rows, a bound that some block reaches. `segments`: never falling along the sequence; each segment holds 1 to 8192 positions, one exactly that many.
All inputs are finite; a program needn't handle non-finite values.
Results may differ from the reference program's by a relative error of at most 0.03.
Values may be sent and summed in bfloat16 or wider, within the bound.
A program may use at most 128 MiB of HBM per device.

```python
import math
import jax
import jax.numpy as jnp
import numpy as np
from jax import lax

D = 2048
FF = 768
KV_HEADS = 4
HD = 128
TOPK = 8
Q_HEADS = 16
SEGS = 4
TOK_DEV = 128
EXPERTS = 128
TOKENS = 16384
CAP = 12
N_EXPERT = 32
N_GROUP = 4


def levels(stream_key, extent, cuts, low, top_value):
    loudness, own = 1.0, jax.random.fold_in(stream_key, 6)
    for position, shards_of in cuts:
        draws = jnp.exp(jax.random.uniform(jax.random.fold_in(own, position), (shards_of,), jnp.float32, low / len(cuts), top_value / len(cuts)))
        loudness = loudness * jnp.repeat(draws, extent[position] // shards_of).reshape([-1 if axis == position else 1 for axis in range(len(extent))])
    return loudness


def profile(number_of, total, reach, skew):
    portions = [(1 << 20) // math.isqrt(grade ** skew) + 1 for grade in range(2, number_of + 1)]
    spare, given = total - reach - (number_of - 1), [1] * (number_of - 1)
    while spare > 0:
        movable = [i for i in range(number_of - 1) if given[i] < reach]
        whole, left = sum([portions[i] for i in movable]), spare
        for i in movable:
            more = min(reach - given[i], max(1, left * portions[i] // whole), spare)
            given[i] = given[i] + more
            spare = spare - more
    return np.array([reach] + given)


def uneven_parts(key, number_of, total, bound, lean):
    if number_of == 2:
        one = jax.random.randint(key, (), max(1, total - bound), min(bound, total - 1) + 1)
        return jnp.stack([one, total - one])
    sizes = jnp.asarray(profile(number_of, total, bound, lean), jnp.int32)
    pairs = (number_of - 1) // 2
    donor, taker = sizes[1:1 + 2 * pairs:2], sizes[2:2 + 2 * pairs:2]
    margin = jnp.minimum(donor - 1, bound - taker)
    moved = jax.random.randint(jax.random.fold_in(key, 1), (pairs,), 0, 1 << 20) % (margin + 1)
    sizes = sizes.at[1:1 + 2 * pairs:2].set(donor - moved).at[2:2 + 2 * pairs:2].set(taker + moved)
    return sizes[jax.random.permutation(jax.random.fold_in(key, 2), number_of)]


def assign_block(own_key, own, number, rows, number_of, top, reach, slope):
    order = jax.random.permutation(own_key, number_of)
    packed, common = shares(number_of, rows * top, reach, slope, True), shares(number_of, rows * top, reach, slope, False)
    places = jnp.arange(number_of)

    def named(sizes, rotation):
        used = int((sizes > 0).sum())
        fixed = max(1, used // 4)
        moved = fixed + (places - fixed + rotation * (used - fixed)) % max(1, number_of - fixed)
        return jnp.zeros((number_of,), jnp.int32).at[order[jnp.where(places < fixed, places, moved)]].set(jnp.asarray(sizes, jnp.int32))

    sizes = jnp.where(number % 4 == 0, named(packed, number // 4), named(common, number - number // 4 - 1))
    mixed = jax.random.permutation(jax.random.fold_in(own, 3), number_of)
    giver, sink = mixed[0:number_of // 2 * 2:2], mixed[1:number_of // 2 * 2:2]
    margin = jnp.minimum(sizes[giver] - 1, reach - sizes[sink]) // 2
    margin = jnp.where((giver == order[0]) | (sink == order[0]) | (sizes[sink] == 0), 0, jnp.maximum(margin, 0))
    moved = jax.random.randint(jax.random.fold_in(own, 4), (number_of // 2,), 0, 1 << 20) % (margin + 1)
    sizes = sizes.at[giver].add(-moved).at[sink].add(moved)
    items = jnp.searchsorted(jnp.cumsum(sizes), jnp.arange(rows * top), side="right").astype(jnp.int32)
    table = items.reshape(top, rows).T
    table = table[jax.random.permutation(jax.random.fold_in(own, 1), rows)]
    rotation = jax.random.randint(jax.random.fold_in(own, 2), (rows, 1), 0, top)
    return jnp.take_along_axis(table, (jnp.arange(top)[None, :] + rotation) % top, axis=1)


def shares(number_of, total, bound, lean, full):
    weights = [(1 << 20) // math.isqrt(grade ** lean) + 1 for grade in range(1, number_of + 1)]
    largest = bound if full else min(bound, max(-(-total // number_of), total * weights[0] // sum(weights)))
    least = 1 if total - largest >= number_of - 1 else 0
    given, spare = [largest] + [least] * (number_of - 1), total - largest - least * (number_of - 1)
    while spare > 0:
        candidates = [i for i in range(1, number_of) if given[i] < largest] or [i for i in range(1, number_of) if given[i] < bound]
        pool, remaining = sum([weights[i] for i in candidates]), spare
        for i in candidates:
            extra = min(bound - given[i], max(1, remaining * weights[i] // pool), spare)
            given[i] = given[i] + extra
            spare = spare - extra
    return np.array(given)


def bell_draw(stream_key, extent, deviation, reach, shards=(), held_as=jnp.bfloat16):
    array = jax.random.normal(stream_key, extent, jnp.float32) * deviation
    if len(shards) > 0:
        array = levels(stream_key, extent, shards, -0.22, 0.18) * array
    return jnp.clip(array, min=-reach, max=reach).astype(held_as)


def setup_inputs(seed: int = 0) -> dict:
    keys = jax.random.split(jax.random.key(seed), 19)
    tokens = bell_draw(keys[0], (TOKENS, D), 1.0, 6.0, ((0, 128),))
    low_tap = bell_draw(keys[1], (TOKENS, D), 1.0, 6.0, ((0, 128),))
    mid_tap = bell_draw(keys[2], (TOKENS, D), 1.0, 6.0, ((0, 128),))
    next_embed = bell_draw(keys[3], (TOKENS, D), 1.0, 6.0, ((0, 128),))
    expert_ids_keys = jax.random.split(jax.random.fold_in(keys[4], 1), TOKENS // TOK_DEV)
    expert_ids_turns = jax.random.permutation(jax.random.fold_in(keys[4], 3), TOKENS // TOK_DEV)
    expert_ids = jax.vmap(lambda own, number: assign_block(jax.random.fold_in(keys[4], 2), own, number, TOK_DEV, EXPERTS, TOPK, CAP, 2))(expert_ids_keys, expert_ids_turns).reshape((TOKENS, TOPK))
    gate_weights = jnp.clip(0.02 + 0.28 * jax.random.uniform(keys[5], (TOKENS, TOPK), jnp.float32) ** levels(keys[5], (TOKENS, TOPK), ((0, 128),), -0.2, 0.2), 0.02, 0.3)
    segments = jnp.searchsorted(jnp.cumsum(uneven_parts(keys[6], SEGS, TOKENS, TOKENS // 2, 0)), jnp.arange(TOKENS), side="right").astype(jnp.int32)
    moe_gain = jnp.clip(1.0 + 0.18 * jax.random.normal(keys[7], (D,), jnp.float32), 0.1, 1.9)
    w_gate = bell_draw(keys[8], (EXPERTS, D, FF), D ** -0.5, 0.125, ((0, 128),))
    w_up = bell_draw(keys[9], (EXPERTS, D, FF), D ** -0.5, 0.125, ((0, 128),))
    w_down = bell_draw(keys[10], (EXPERTS, FF, D), FF ** -0.5, 0.21875, ((0, 128),))
    merge_weight = bell_draw(keys[11], (3 * D, D), (3 * D) ** -0.5, 0.078125, ((1, 4),))
    embed_gain = jnp.clip(1.0 + 0.18 * jax.random.normal(keys[12], (D,), jnp.float32), 0.1, 1.9)
    merged_gain = jnp.clip(1.0 + 0.18 * jax.random.normal(keys[13], (D,), jnp.float32), 0.1, 1.9)
    w_query = bell_draw(keys[14], (2 * D, Q_HEADS * HD), (2 * D) ** -0.5, 0.09375, ((1, 4),))
    w_kv = bell_draw(keys[15], (2 * D, 2, KV_HEADS * HD), (2 * D) ** -0.5, 0.09375, ((2, 4),))
    q_gain = jnp.clip(jax.random.uniform(keys[16], (HD,), jnp.float32, 2.0, 3.0), 2.0, 3.0)
    k_gain = jnp.clip(jax.random.uniform(keys[17], (HD,), jnp.float32, 2.0, 3.0), 2.0, 3.0)
    return dict(tokens=tokens, low_tap=low_tap, mid_tap=mid_tap, next_embed=next_embed, expert_ids=expert_ids, gate_weights=gate_weights, segments=segments, moe_gain=moe_gain, w_gate=w_gate, w_up=w_up, w_down=w_down, merge_weight=merge_weight, embed_gain=embed_gain, merged_gain=merged_gain, w_query=w_query, w_kv=w_kv, q_gain=q_gain, k_gain=k_gain)


EPSILON = 1e-06
THETA = 1000000.0

def rms_scale(values, gain):
    values = values.astype(jnp.float32)
    return values * lax.rsqrt(lax.optimization_barrier(jnp.mean(values * values, axis=-1, keepdims=True)) + EPSILON) * gain

def rotate(values, positions):
    half = values.shape[-1] // 2
    freqs = jnp.power(THETA, -jnp.arange(half, dtype=jnp.float32) * 2.0 / values.shape[-1])
    angles = positions.astype(jnp.float32)[:, None] * freqs[None, :]
    cosine = jnp.concatenate([jnp.cos(angles), jnp.cos(angles)], axis=-1)[:, None, :]
    sine = jnp.concatenate([jnp.sin(angles), jnp.sin(angles)], axis=-1)[:, None, :]
    turned = jnp.concatenate([-values[..., half:], values[..., :half]], axis=-1)
    return values * cosine + turned * sine

def segment_positions(segments):
    labels = jnp.arange(SEGS, dtype=jnp.int32)
    member = (segments[:, None] == labels[None, :]).astype(jnp.int32)
    counts = lax.optimization_barrier(jnp.sum(member, axis=0))
    starts = jnp.cumsum(counts) - counts
    return jnp.arange(segments.shape[0], dtype=jnp.int32) - lax.optimization_barrier(jnp.sum(member * starts[None, :], axis=1))

def expert_ffn(rows, gate_mat, up_mat, down_mat):
    gate = jnp.dot(rows, gate_mat, preferred_element_type=jnp.float32)
    up = jnp.dot(rows, up_mat, preferred_element_type=jnp.float32)
    hidden = (jax.nn.silu(gate) * up).astype(jnp.bfloat16)
    return jnp.dot(hidden, down_mat, preferred_element_type=jnp.float32).astype(jnp.bfloat16)

def reference(tokens, low_tap, mid_tap, next_embed, expert_ids, gate_weights, segments, moe_gain, w_gate, w_up, w_down, merge_weight, embed_gain, merged_gain, w_query, w_kv, q_gain, k_gain):
    slots = N_EXPERT * N_GROUP * CAP
    normed = rms_scale(tokens, moe_gain).astype(jnp.bfloat16)

    def one_expert(total, index):
        hit = expert_ids == index
        share = lax.optimization_barrier(jnp.sum(jnp.where(hit, gate_weights, 0.0), axis=1))
        chosen = jnp.any(hit, axis=1)
        rows = jnp.nonzero(chosen, size=slots, fill_value=0)[0]
        live = jnp.arange(slots) < jnp.sum(chosen.astype(jnp.int32))
        answer = expert_ffn(normed[rows], w_gate[index], w_up[index], w_down[index])
        scaled = jnp.where(live, share[rows], 0.0)[:, None] * answer.astype(jnp.float32)
        return (total.at[rows].add(scaled), None)
    mixed, _ = lax.scan(one_expert, jnp.zeros((TOKENS, D), jnp.float32), jnp.arange(EXPERTS, dtype=jnp.int32))
    high = (tokens.astype(jnp.float32) + mixed).astype(jnp.bfloat16)
    stacked = jnp.concatenate([low_tap, mid_tap, high], axis=1)
    merged = jnp.dot(stacked, merge_weight, preferred_element_type=jnp.float32).astype(jnp.bfloat16)
    joined = jnp.concatenate([rms_scale(next_embed, embed_gain), rms_scale(merged, merged_gain)], axis=1).astype(jnp.bfloat16)
    positions = segment_positions(segments)
    query = jnp.dot(joined, w_query, preferred_element_type=jnp.float32).reshape(TOKENS, Q_HEADS, HD)
    query = rotate(rms_scale(query, q_gain), positions).astype(jnp.bfloat16)
    key = jnp.dot(joined, w_kv[:, 0, :], preferred_element_type=jnp.float32).reshape(TOKENS, KV_HEADS, HD)
    key = rotate(rms_scale(key, k_gain), positions).astype(jnp.bfloat16)
    value = jnp.dot(joined, w_kv[:, 1, :], preferred_element_type=jnp.float32).astype(jnp.bfloat16).reshape(TOKENS, KV_HEADS, HD)
    per_kv = Q_HEADS // KV_HEADS
    block = TOK_DEV * N_GROUP
    count = TOKENS // block
    scale = HD ** (-0.5)
    grouped = query.reshape(count, block, KV_HEADS, per_kv, HD)
    key_index = jnp.arange(TOKENS, dtype=jnp.int32)

    def one_block(item):
        index, queries = item
        query_index = index * block + jnp.arange(block, dtype=jnp.int32)
        query_seg = lax.dynamic_slice_in_dim(segments, index * block, block)
        allowed = (key_index[None, :] <= query_index[:, None]) & (segments[None, :] == query_seg[:, None])

        def one_head(head):
            q_head = lax.dynamic_index_in_dim(queries, head, 1, keepdims=False)
            k_head = lax.dynamic_index_in_dim(key, head, 1, keepdims=False)
            v_head = lax.dynamic_index_in_dim(value, head, 1, keepdims=False)
            scores = jnp.einsum('qgd,kd->gqk', q_head.astype(jnp.float32), k_head.astype(jnp.float32)) * scale
            weights = jnp.where(allowed[None], jnp.exp(scores), 0.0)
            rounded = lax.optimization_barrier(weights.astype(jnp.bfloat16)).astype(jnp.float32)
            total = jnp.einsum('gqk,kd->gqd', rounded, v_head.astype(jnp.float32))
            return total / lax.optimization_barrier(jnp.sum(weights, axis=-1))[..., None]
        heads = lax.map(one_head, jnp.arange(KV_HEADS, dtype=jnp.int32))
        return jnp.transpose(heads, (2, 0, 1, 3)).reshape(block, Q_HEADS * HD)
    result = lax.map(one_block, (jnp.arange(count, dtype=jnp.int32), grouped))
    return result.reshape(TOKENS, Q_HEADS * HD).astype(jnp.bfloat16)
```

```python
import jax
import jax.numpy as jnp
from jax import lax
from jax.experimental import pallas as pl
from jax.experimental.pallas import tpu as pltpu
from jax.sharding import PartitionSpec as P

D = 2048
HD = 128
TOPK = 8
SEGS = 4


EPSILON = 1e-06
THETA = 1000000.0
LOG2E = 1.4426950408889634


def rms_scale(values, gain):
    values = values.astype(jnp.float32)
    return values * lax.rsqrt(jnp.mean(values * values, axis=-1, keepdims=True) + EPSILON) * gain


def rotate(values, positions):
    half = values.shape[-1] // 2
    freqs = jnp.power(THETA, -jnp.arange(half, dtype=jnp.float32) * 2.0 / values.shape[-1])
    angles = positions.astype(jnp.float32)[:, None] * freqs[None, :]
    cosine = jnp.concatenate([jnp.cos(angles), jnp.cos(angles)], axis=-1)[:, None, :]
    sine = jnp.concatenate([jnp.sin(angles), jnp.sin(angles)], axis=-1)[:, None, :]
    turned = jnp.concatenate([-values[..., half:], values[..., :half]], axis=-1)
    return values * cosine + turned * sine


def segment_positions(segments):
    labels = jnp.arange(SEGS, dtype=jnp.int32)
    member = (segments[:, None] == labels[None, :]).astype(jnp.int32)
    counts = jnp.sum(member, axis=0)
    starts = jnp.cumsum(counts) - counts
    return jnp.arange(segments.shape[0], dtype=jnp.int32) - jnp.sum(
        member * starts[None, :], axis=1
    )


def expert_ffn(rows, gate_mat, up_mat, down_mat):
    gate = jnp.dot(rows, gate_mat, preferred_element_type=jnp.float32)
    up = jnp.dot(rows, up_mat, preferred_element_type=jnp.float32)
    hidden = (jax.nn.silu(gate) * up).astype(jnp.bfloat16)
    return jnp.dot(hidden, down_mat, preferred_element_type=jnp.float32).astype(jnp.bfloat16)


def attend_kernel(bounds, query, pairs, row_start, out, total):
    heads, rows, _ = query.shape
    first_start, low, mine = bounds[0], bounds[1], bounds[2]
    total[...] = jnp.zeros_like(total)

    def add_block(index, masked):
        key = pairs[index, 0]
        value = jnp.concatenate([pairs[index, 1], jnp.ones((rows, HD), jnp.bfloat16)], axis=1)
        if masked:
            row = mine * rows + lax.broadcasted_iota(jnp.int32, (rows, rows), 0)
            col = index * rows + lax.broadcasted_iota(jnp.int32, (rows, rows), 1)
            allowed = (col <= row) & (col >= row_start[...])
        for head in range(heads):
            scores = lax.dot_general(
                query[head], key, (((1,), (1,)), ((), ())), preferred_element_type=jnp.float32
            )
            weights = jnp.exp2(scores)
            if masked:
                weights = jnp.where(allowed, weights, 0.0)
            total[head] += jnp.dot(
                weights.astype(jnp.bfloat16), value, preferred_element_type=jnp.float32
            )

    @pl.loop(low + 1, mine)
    def _(index):
        add_block(index, False)

    same = row_start[...] == first_start
    for head in range(heads):
        total[head] = jnp.where(same, total[head], 0.0)

    @pl.loop(0, jnp.where(low < mine, 2, 1))
    def _(index):
        add_block(jnp.where(index == 0, mine, low), True)

    for head in range(heads):
        out[:, head * HD : (head + 1) * HD] = (
            total[head, :, :HD] / total[head, :, HD:]
        ).astype(out.dtype)


def attend(bounds, query, pairs, row_start):
    rows, heads, _ = query.shape
    vmem = pl.BlockSpec(memory_space=pltpu.VMEM)
    return pl.pallas_call(
        attend_kernel,
        out_shape=jax.ShapeDtypeStruct((rows, heads * HD), jnp.bfloat16),
        in_specs=[pl.BlockSpec(memory_space=pltpu.SMEM), vmem, vmem, vmem],
        out_specs=vmem,
        scratch_shapes=[pltpu.VMEM((heads, rows, 2 * HD), jnp.float32)],
        compiler_params=pltpu.CompilerParams(vmem_limit_bytes=48 << 20),
        name="attend",
    )(bounds, jnp.transpose(query, (1, 0, 2)), pairs, row_start)


def body(
    tokens,
    low_tap,
    mid_tap,
    next_embed,
    expert_ids,
    gate_weights,
    segments,
    moe_gain,
    w_gate,
    w_up,
    w_down,
    merge_weight,
    embed_gain,
    merged_gain,
    w_query,
    w_kv,
    q_gain,
    k_gain,
):
    n_expert = lax.axis_size("expert")
    n_group = lax.axis_size("group")
    devices = n_expert * n_group
    tok_rows = tokens.shape[0]
    capacity = 3 * tok_rows * TOPK // (2 * devices)
    normed = rms_scale(tokens, moe_gain).astype(jnp.bfloat16)
    flat_ids = expert_ids.reshape(-1)
    picks = flat_ids.shape[0]
    onehot = (flat_ids[:, None] == jnp.arange(devices, dtype=jnp.int32)[None, :]).astype(
        jnp.bfloat16
    )
    order = jnp.arange(picks, dtype=jnp.int32)
    earlier = (order[:, None] > order[None, :]).astype(jnp.bfloat16)
    ranks = jnp.dot(earlier, onehot, preferred_element_type=jnp.float32)
    slot_of = jnp.sum(ranks * onehot.astype(jnp.float32), axis=1).astype(jnp.int32)
    target = flat_ids * capacity + slot_of
    place = jnp.arange(devices * capacity, dtype=jnp.int32)[:, None] == target[None, :]
    place = jnp.any(place.reshape(devices * capacity, tok_rows, TOPK), axis=2).astype(jnp.bfloat16)
    packed = jnp.dot(place, normed, preferred_element_type=jnp.float32).astype(jnp.bfloat16)
    packed = packed.reshape(devices, capacity, D)
    items = lax.all_to_all(packed, ("expert", "group"), split_axis=0, concat_axis=0, tiled=True)
    rows = items.reshape(-1, items.shape[-1])
    answered = expert_ffn(rows, w_gate[0], w_up[0], w_down[0]).reshape(items.shape)
    returned = lax.all_to_all(
        answered, ("expert", "group"), split_axis=0, concat_axis=0, tiled=True
    )
    returned = returned.reshape(devices * capacity, D)
    picked = jnp.take(returned, target, axis=0).reshape(tok_rows, TOPK, D)
    mixed = jnp.einsum("tkd,tk->td", picked, gate_weights, preferred_element_type=jnp.float32)
    high = (tokens.astype(jnp.float32) + mixed).astype(jnp.bfloat16)
    low_rows, mid_rows, high_rows, embed_rows = (
        lax.all_gather(low_tap, "group", axis=0, tiled=True),
        lax.all_gather(mid_tap, "group", axis=0, tiled=True),
        lax.all_gather(high, "group", axis=0, tiled=True),
        lax.all_gather(next_embed, "group", axis=0, tiled=True),
    )
    stacked = jnp.concatenate([low_rows, mid_rows, high_rows], axis=1)
    merged_part = jnp.dot(stacked, merge_weight, preferred_element_type=jnp.float32).astype(
        jnp.bfloat16
    )
    merged = lax.all_gather(merged_part, "group", axis=1, tiled=True)
    joined = jnp.concatenate(
        [rms_scale(embed_rows, embed_gain), rms_scale(merged, merged_gain)], axis=1
    ).astype(jnp.bfloat16)
    block_rows = joined.shape[0]
    first = lax.axis_index("expert") * block_rows
    every_position = segment_positions(segments)
    my_positions = lax.dynamic_slice_in_dim(every_position, first, block_rows)
    my_segments = lax.dynamic_slice_in_dim(segments, first, block_rows)
    row_index = first + jnp.arange(block_rows, dtype=jnp.int32)
    query = jnp.dot(joined, w_query, preferred_element_type=jnp.float32).reshape(block_rows, -1, HD)
    query = rotate(rms_scale(query, q_gain), my_positions)
    key = jnp.dot(joined, w_kv[:, 0, :], preferred_element_type=jnp.float32).reshape(
        block_rows, -1, HD
    )
    key = rotate(rms_scale(key, k_gain), my_positions).astype(jnp.bfloat16)
    value = jnp.dot(joined, w_kv[:, 1, :], preferred_element_type=jnp.float32).astype(jnp.bfloat16)
    scale = HD ** (-0.5) * LOG2E
    scaled = (query * scale).astype(jnp.bfloat16)
    paired = jnp.stack([key.reshape(block_rows, HD), value], axis=0)
    gathered = lax.all_gather(paired, "expert", axis=0)
    row_start = (row_index - my_positions)[:, None]
    bounds = jnp.stack([row_start[0, 0], row_start[0, 0] // block_rows, lax.axis_index("expert")])
    return attend(bounds, scaled, gathered, row_start)


def solution(mesh):
    return jax.shard_map(
        body,
        mesh=mesh,
        in_specs=(
            P(("expert", "group"), None),
            P(("expert", "group"), None),
            P(("expert", "group"), None),
            P(("expert", "group"), None),
            P(("expert", "group"), None),
            P(("expert", "group"), None),
            P(),
            P(),
            P(("expert", "group"), None, None),
            P(("expert", "group"), None, None),
            P(("expert", "group"), None, None),
            P(None, "group"),
            P(),
            P(),
            P(None, "group"),
            P(None, None, "group"),
            P(),
            P(),
        ),
        out_specs=P("expert", "group"),
        check_vma=False,
    )
```

```python
import jax
import jax.numpy as jnp
from jax import lax
from jax.experimental import pallas as pl
from jax.experimental.pallas import tpu as pltpu
from jax.sharding import PartitionSpec as P

D = 2048
HD = 128
TOPK = 8
SEGS = 4


EPSILON = 1e-06
THETA = 1000000.0
LOG2E = 1.4426950408889634
MESH = pl.DeviceIdType.MESH
N_Z, N_Y, N_CORE, N_X = 4, 4, 2, 4
PEERS = N_Z * N_Y * N_CORE
ROUND = 8
WINDOW = 16
CUTS = 4
CAPACITY = 12
NOWHERE = -1000.0


def offset_of(slot):
    turn = slot // N_CORE
    return ((turn // N_Y + turn) % N_Z, turn % N_Y, slot % N_CORE)


def peer(offset, sign=1):
    here = lax.axis_index("expert")
    z = (here // (N_Y * N_CORE) + sign * offset[0] + N_Z) % N_Z
    y = (here // N_CORE % N_Y + sign * offset[1] + N_Y) % N_Y
    core = (here + offset[2]) % N_CORE
    return (z * N_Y + y) * N_CORE + core


def remote(source, target, sends, arrivals, slot, device):
    return pltpu.make_async_remote_copy(
        src_ref=source,
        dst_ref=target,
        send_sem=sends.at[slot],
        recv_sem=arrivals.at[slot],
        device_id=device,
        device_id_type=MESH,
    )


def greet(devices):
    barrier = pltpu.get_barrier_semaphore()
    for device in devices:
        pl.semaphore_signal(barrier, inc=1, device_id=device, device_id_type=MESH)
    pl.semaphore_wait(barrier, len(devices))


def across(step):
    return (lax.axis_index("expert"), (lax.axis_index("group") + step) % N_X)


def experts_kernel(
    tokens, routing, low, mid, embed, w_gate, w_up, w_down, w_merge, gain,
    merged, embed_rows,
    route, place, weights, shares, all_tokens, packed, arrived, normed, hidden, returned,
    total, partial, halves, high, low_rows, mid_rows, merge_total,
    gate_mat, up_mat, down_mat, merge_mat,
    own, route_sends, route_arrivals, token_sends, token_arrivals, out_sends, out_arrivals,
    back_sends, back_arrivals, tap_sends, tap_arrivals, sum_sends, sum_arrivals,
    high_sends, high_arrivals,
):
    x = lax.axis_index("group")
    rows = tokens.shape[0]
    slots = CAPACITY * N_X
    batch = ROUND * slots
    batches = PEERS // ROUND
    cut = D // CUTS
    steps = range(1, N_X)
    mine = pl.ds(pl.multiple_of(x * rows, rows), rows)

    def columns(part):
        return pl.ds(pl.multiple_of(part * cut, cut), cut)

    def slot_rows(slot):
        return pl.ds(pl.multiple_of(slot * slots, slots), slots)

    def batch_rows(index):
        return pl.ds(pl.multiple_of(index * batch, batch), batch)

    kept = [
        pltpu.make_async_copy(source, target, own.at[index])
        for index, (source, target) in enumerate(
            (
                (routing.at[x], route.at[x]),
                (tokens, all_tokens.at[mine]),
                (w_gate, gate_mat),
                (w_up, up_mat),
                (w_down, down_mat),
                (low, low_rows.at[mine]),
                (mid, mid_rows.at[mine]),
                (w_merge, merge_mat),
                (embed, embed_rows.at[mine]),
            )
        )
    ]
    for copy in kept:
        copy.start()

    barrier = pltpu.get_barrier_semaphore()
    for step in steps:
        pl.semaphore_signal(barrier, inc=1, device_id=across(step), device_id_type=MESH)

    @pl.loop(1, PEERS)
    def _(slot):
        pl.semaphore_signal(
            barrier, inc=1, device_id=(peer(offset_of(slot), -1), x), device_id_type=MESH
        )

    pl.semaphore_wait(barrier, PEERS - 1 + N_X - 1)

    def route_copy(step):
        return remote(
            routing.at[(x + step) % N_X], route.at[x], route_sends, route_arrivals, step - 1,
            across(step),
        )

    def token_copy(part, step):
        return remote(
            tokens.at[:, columns(part)], all_tokens.at[mine, columns(part)],
            token_sends, token_arrivals, (N_X - 1) * part + step - 1, across(step),
        )

    def outward(slot, part):
        return remote(
            packed.at[slot_rows(slot), columns(part)], arrived.at[slot_rows(slot), columns(part)],
            out_sends, out_arrivals, PEERS * part + slot, (peer(offset_of(slot)), x),
        )

    def homeward(slot, part):
        return remote(
            packed.at[slot_rows(slot), columns(part)], returned.at[slot_rows(slot), columns(part)],
            back_sends, back_arrivals, PEERS * part + slot, (peer(offset_of(slot), -1), x),
        )

    def tap_copy(index, step):
        source = (low, mid, embed)[index]
        target = (low_rows, mid_rows, embed_rows)[index]
        return remote(
            source, target.at[mine], tap_sends, tap_arrivals, (N_X - 1) * index + step - 1,
            across(step),
        )

    def sum_copy(part, step):
        theirs = pl.ds(pl.multiple_of((x + step) % N_X * rows, rows), rows)
        return remote(
            partial.at[theirs, columns(part)], halves.at[step - 1, :, columns(part)],
            sum_sends, sum_arrivals, (N_X - 1) * part + step - 1, across(step),
        )

    def high_copy(part, step):
        return remote(
            high.at[mine, columns(part)], high.at[mine, columns(part)],
            high_sends, high_arrivals, (N_X - 1) * part + step - 1, across(step),
        )

    for step in steps:
        route_copy(step).start()
    for part in range(CUTS):
        for step in steps:
            token_copy(part, step).start()
    kept[0].wait()
    for step in steps:
        route_copy(step).wait_recv()

    @pl.loop(0, batches)
    def _(index):
        @pl.loop(0, ROUND)
        def _(inner):
            slot = index * ROUND + inner
            spots = jnp.concatenate(
                [route[block, 0, pl.ds(slot, 1), :] for block in range(N_X)], axis=1
            )
            share = jnp.concatenate(
                [route[block, 1, pl.ds(slot, 1), :] for block in range(N_X)], axis=1
            )
            lines = lax.broadcasted_iota(jnp.int32, (slots, N_X * rows), 0).astype(jnp.float32)
            match = lines == spots
            place[slot_rows(slot), :] = jnp.where(match, 1.0, 0.0).astype(jnp.bfloat16)
            weights[slot_rows(inner), :] = jnp.where(match, share, 0.0)

        shares[:, batch_rows(index)] = weights[...].T.astype(jnp.bfloat16)

    kept[1].wait()

    @pl.loop(0, CUTS)
    def _(part):
        for step in steps:
            token_copy(part, step).wait_recv()

        @pl.loop(0, batches)
        def _(index):
            span = batch_rows(index)
            packed[span, columns(part)] = jnp.dot(
                place[span, :], all_tokens[:, columns(part)], preferred_element_type=jnp.float32
            ).astype(jnp.bfloat16)

            @pl.loop(index * ROUND, (index + 1) * ROUND)
            def _(slot):
                pl.when(slot > 0)(lambda: outward(slot, part).start())

        arrived[slot_rows(0), columns(part)] = packed[slot_rows(0), columns(part)]

    for index in range(3):
        for step in steps:
            tap_copy(index, step).start()
    for copy in kept[2:]:
        copy.wait()

    def reply(index, part):
        span = batch_rows(index)
        packed[span, columns(part)] = jnp.dot(
            hidden[span, :], down_mat[:, columns(part)], preferred_element_type=jnp.float32
        ).astype(jnp.bfloat16)

        @pl.loop(index * ROUND, (index + 1) * ROUND)
        def _(slot):
            pl.when(slot > 0)(lambda: homeward(slot, part).start())

        @pl.when(index == 0)
        def _():
            returned[slot_rows(0), columns(part)] = packed[slot_rows(0), columns(part)]

    def each_copy(index, act):
        @pl.loop(0, ROUND * CUTS)
        def _(inner):
            slot = index * ROUND + inner % ROUND
            pl.when(slot > 0)(lambda: act(slot, inner // ROUND))

    @pl.loop(0, batches)
    def _(index):
        each_copy(index, lambda slot, part: outward(slot, part).wait_recv())

        @pl.loop(0, ROUND)
        def _(inner):
            values = arrived[slot_rows(index * ROUND + inner), :].astype(jnp.float32)
            size = lax.rsqrt(jnp.mean(values * values, axis=-1, keepdims=True) + EPSILON)
            normed[slot_rows(inner), :] = (values * size * gain[...]).astype(jnp.bfloat16)

        @pl.loop(0, w_gate.shape[1] // 256)
        def _(tile):
            tiles = pl.ds(pl.multiple_of(tile * 256, 256), 256)
            gate = jnp.dot(normed[...], gate_mat[:, tiles], preferred_element_type=jnp.float32)
            up = jnp.dot(normed[...], up_mat[:, tiles], preferred_element_type=jnp.float32)
            hidden[batch_rows(index), tiles] = (gate / (1.0 + jnp.exp(-gate)) * up).astype(
                jnp.bfloat16
            )

        each_copy(index, lambda slot, part: outward(slot, part).wait_send())
        reply(index, 0)

    @pl.loop(batches, CUTS * batches)
    def _(turn):
        reply(turn % batches, turn // batches)

    for index in range(2):
        for step in steps:
            tap_copy(index, step).wait_recv()
    merge_total[...] = jnp.zeros_like(merge_total)

    def add_merge(source, index, part):
        depth = pl.ds(pl.multiple_of(index * D + part * cut, cut), cut)
        merge_total[...] += jnp.dot(
            source[:, columns(part)], merge_mat[depth, :], preferred_element_type=jnp.float32
        )

    @pl.loop(0, CUTS)
    def _(part):
        add_merge(low_rows, 0, part)
        add_merge(mid_rows, 1, part)

    def add_high(part):
        for step in steps:
            high_copy(part, step).wait_recv()
        add_merge(high, 2, part)

    @pl.loop(0, CUTS)
    def _(part):
        total[...] = jnp.zeros_like(total)

        @pl.loop(0, batches)
        def _(index):
            @pl.loop(index * ROUND, (index + 1) * ROUND)
            def _(slot):
                pl.when(slot > 0)(lambda: homeward(slot, part).wait_recv())

            span = batch_rows(index)
            total[...] += jnp.dot(
                shares[:, span], returned[span, columns(part)], preferred_element_type=jnp.float32
            )

        partial[:, columns(part)] = total[...].astype(jnp.bfloat16)
        for step in steps:
            sum_copy(part, step).start()
        mixed = all_tokens[mine, columns(part)].astype(jnp.float32) + total[mine, :]
        for step in steps:
            sum_copy(part, step).wait_recv()
            mixed += halves[step - 1, :, columns(part)].astype(jnp.float32)
        high[mine, columns(part)] = mixed.astype(jnp.bfloat16)
        for step in steps:
            high_copy(part, step).start()
        pl.when(part > 0)(lambda: add_high(part - 1))

    add_high(CUTS - 1)
    merged[...] = merge_total[...].astype(jnp.bfloat16)

    @pl.loop(0, batches)
    def _(index):
        each_copy(index, lambda slot, part: homeward(slot, part).wait_send())

    for step in steps:
        route_copy(step).wait_send()
        tap_copy(2, step).wait_recv()
        for index in range(3):
            tap_copy(index, step).wait_send()

        @pl.loop(0, CUTS)
        def _(part):
            token_copy(part, step).wait_send()
            sum_copy(part, step).wait_send()
            high_copy(part, step).wait_send()


def experts(tokens, routing, low, mid, embed, w_gate, w_up, w_down, w_merge, gain):
    rows, width, out_width = tokens.shape[0], w_gate.shape[1], w_merge.shape[1]
    everyone = N_X * rows
    slots = CAPACITY * N_X
    hbm = pl.BlockSpec(memory_space=pl.ANY)
    vmem = pl.BlockSpec(memory_space=pltpu.VMEM)
    dma = pltpu.SemaphoreType.DMA

    def half(*shape):
        return pltpu.VMEM(shape, jnp.bfloat16)

    def full(*shape):
        return pltpu.VMEM(shape, jnp.float32)

    few, many = (N_X - 1) * CUTS, PEERS * CUTS
    return pl.pallas_call(
        experts_kernel,
        out_shape=(
            jax.ShapeDtypeStruct((everyone, out_width), jnp.bfloat16),
            jax.ShapeDtypeStruct((everyone, D), jnp.bfloat16),
        ),
        in_specs=[hbm] * 9 + [vmem],
        out_specs=(vmem, hbm),
        scratch_shapes=[
            full(N_X, 2, PEERS, rows),
            half(PEERS * slots, everyone),
            full(ROUND * slots, everyone),
            half(everyone, PEERS * slots),
            half(everyone, D),
            half(PEERS * slots, D),
            half(PEERS * slots, D),
            half(ROUND * slots, D),
            half(PEERS * slots, width),
            half(PEERS * slots, D),
            full(everyone, D // CUTS),
            half(everyone, D),
            half(N_X - 1, rows, D),
            half(everyone, D),
            half(everyone, D),
            half(everyone, D),
            full(everyone, out_width),
            half(D, width),
            half(D, width),
            half(width, D),
            half(3 * D, out_width),
            dma((9,)),
            dma((N_X - 1,)), dma((N_X - 1,)),
            dma((few,)), dma((few,)),
            dma((many,)), dma((many,)),
            dma((many,)), dma((many,)),
            dma((9,)), dma((9,)),
            dma((few,)), dma((few,)),
            dma((few,)), dma((few,)),
        ],
        compiler_params=pltpu.CompilerParams(
            collective_id=2, has_side_effects=True, vmem_limit_bytes=60 << 20
        ),
        cost_estimate=pl.CostEstimate(
            flops=6 * PEERS * slots * D * width, bytes_accessed=40 << 20, transcendentals=0
        ),
        name="experts",
    )(tokens, routing, low, mid, embed, w_gate, w_up, w_down, w_merge, gain)


def rotation(positions):
    half = HD // 2
    freqs = jnp.power(THETA, -jnp.arange(half, dtype=jnp.float32) * 2.0 / HD)
    angles = positions.astype(jnp.float32)[:, None] * freqs[None, :]
    cosine, sine = jnp.cos(angles), jnp.sin(angles)
    return jnp.concatenate([cosine, cosine], axis=1), jnp.concatenate([-sine, sine], axis=1)


def segment_positions(segments):
    labels = jnp.arange(SEGS, dtype=jnp.int32)
    member = (segments[:, None] == labels[None, :]).astype(jnp.int32)
    counts = jnp.sum(member, axis=0)
    starts = jnp.cumsum(counts) - counts
    return jnp.arange(segments.shape[0], dtype=jnp.int32) - jnp.sum(
        member * starts[None, :], axis=1
    )


def draft_kernel(
    merged, embed, w_query, w_kv, embed_gain, merged_gain, q_gain, k_gain, cosine, sine, row_start,
    out,
    pieces, embeds, joined, embed_total, merged_total, squares, query, held, total,
    query_mat, kv_mat,
    x_sends, x_arrivals, z_sends, z_arrivals, y_sends, y_arrivals, core_sends, core_arrivals, own,
):
    rows, cut = merged.shape
    heads = query.shape[0]
    here, x = lax.axis_index("expert"), lax.axis_index("group")
    z, y, core = here // (N_Y * N_CORE), here // N_CORE % N_Y, here % N_CORE
    loads = [
        pltpu.make_async_copy(source, target, own.at[index])
        for index, (source, target) in enumerate(
            ((merged, pieces.at[x]), (embed, embeds), (w_query, query_mat), (w_kv, kv_mat))
        )
    ]
    for load in loads:
        load.start()
    greet(
        [across(step) for step in (1, 2, 3)]
        + [(peer((step, 0, 0)), x) for step in (1, 2, 3)]
        + [(peer((0, step, 0)), x) for step in (1, 2, 3)]
        + [(peer((0, 0, 1)), x)]
    )
    near, far = 1, N_X - 1
    halves = (pl.ds(0, rows // 2), pl.ds(rows // 2, rows // 2))

    def direct(index):
        return remote(
            merged, pieces.at[x], x_sends, x_arrivals, index, across((near, far)[index])
        )

    def onward(index):
        block = (x + (far, near)[index]) % N_X
        span = halves[index]
        return remote(
            pieces.at[block, span], pieces.at[block, span], x_sends, x_arrivals, 2 + index,
            across((near, far)[index]),
        )

    for index in (0, 1):
        direct(index).start()

    def add_part(source, depth, target):
        target[:, : heads * HD] += jnp.dot(
            source, query_mat[depth, :], preferred_element_type=jnp.float32
        )
        target[:, heads * HD :] += jnp.dot(
            source, kv_mat[depth, :], preferred_element_type=jnp.float32
        )

    def columns(part):
        return pl.ds(pl.multiple_of(part * cut, cut), cut)

    embed_total[...] = jnp.zeros_like(embed_total)
    merged_total[...] = jnp.zeros_like(merged_total)
    squares[...] = jnp.zeros_like(squares)
    loads[1].wait()
    chunk = rows // 8

    @pl.loop(0, 8)
    def _(index):
        span = pl.ds(pl.multiple_of(index * chunk, chunk), chunk)
        values = embeds[span, :].astype(jnp.float32)
        size = lax.rsqrt(jnp.mean(values * values, axis=-1, keepdims=True) + EPSILON)
        joined[span, :] = (values * size * embed_gain[...]).astype(jnp.bfloat16)

    for load in (loads[0], loads[2], loads[3]):
        load.wait()

    @pl.loop(0, N_X)
    def _(part):
        add_part(joined[:, columns(part)], columns(part), embed_total)

    def add_piece(block):
        values = pieces[block].astype(jnp.float32)
        squares[...] += jnp.broadcast_to(
            jnp.sum(values * values, axis=-1, keepdims=True), squares.shape
        )
        source = (values * merged_gain[:, columns(block)]).astype(jnp.bfloat16)
        add_part(source, pl.ds(pl.multiple_of(D + block * cut, cut), cut), merged_total)

    for index in (0, 1):
        direct(index).wait_recv()
        onward(index).start()

    @pl.loop(0, N_X)
    def _(turn):
        @pl.when(turn == N_X - 1)
        def _():
            for index in (0, 1):
                onward(index).wait_recv()

        add_piece((x + jnp.where(turn == 3, 2, jnp.where(turn == 2, 3, turn))) % N_X)

    shrink = lax.rsqrt(squares[:, :1] * (1.0 / D) + EPSILON)

    def project(index):
        span = slice(index * HD, (index + 1) * HD)
        return embed_total[:, span] + merged_total[:, span] * shrink

    def turned(values, gain):
        size = lax.rsqrt(jnp.mean(values * values, axis=-1, keepdims=True) + EPSILON)
        values = values * size * gain[...]
        return values * cosine[...] + pltpu.roll(values, HD // 2, 1) * sine[...]

    for index in range(heads):
        query[index] = (turned(project(index), q_gain) * (HD**-0.5 * LOG2E)).astype(jnp.bfloat16)

    def place(plane, row, column):
        return (plane * N_Y + row) * N_CORE + column

    def wanted(plane, row, reader):
        near = (plane == 0) & (row <= reader)
        return near | ((plane == 1) & (z >= 1)) | ((plane == 2) & (z >= 2) & (row >= reader))

    def along_z(plane):
        return remote(
            held.at[place(0, y, core)], held.at[place(plane, y, core)], z_sends, z_arrivals,
            plane - 1,
            (peer((plane, 0, 0)), x),
        )

    def along_y(plane, step):
        slot = place(plane, y, core)
        return remote(
            held.at[slot], held.at[slot], y_sends, y_arrivals, 3 * plane + step - 1,
            (peer((0, step, 0)), x),
        )

    def to_sibling(plane, row):
        slot = place(plane, row, core)
        return remote(
            held.at[slot], held.at[slot], core_sends, core_arrivals, N_Y * plane + row,
            (peer((0, 0, 1)), x),
        )

    def from_sibling(plane, row):
        slot = place(plane, row, 1 - core)
        return remote(
            held.at[slot], held.at[slot], core_sends, core_arrivals, N_Y * plane + row,
            (peer((0, 0, 1)), x),
        )

    def share(plane):
        for step in (1, 2, 3):
            pl.when(wanted(plane, y, (y + step) % N_Y))(along_y(plane, step).start)

    held[place(0, y, core), 0] = turned(project(heads), k_gain).astype(jnp.bfloat16)
    held[place(0, y, core), 1] = project(heads + 1).astype(jnp.bfloat16)
    for plane in (1, 2):
        pl.when(z + plane < N_Z)(along_z(plane).start)
    total[...] = jnp.zeros_like(total)
    share(0)
    to_sibling(0, y).start()

    def add_block(plane, row, column):
        slot = place(plane, row, column)
        first = ((z - plane) * N_Y * N_CORE + row * N_CORE + column) * rows
        key = held[slot, 0]
        value = jnp.concatenate([held[slot, 1], jnp.ones((rows, HD), jnp.bfloat16)], axis=1)
        query_index = here * rows + lax.broadcasted_iota(jnp.int32, (rows, rows), 0)
        key_index = first + lax.broadcasted_iota(jnp.int32, (rows, rows), 1)
        allowed = (key_index <= query_index) & (key_index >= row_start[...])
        for head in range(heads):
            scores = lax.dot_general(
                query[head], key, (((1,), (1,)), ((), ())), preferred_element_type=jnp.float32
            )
            weights = jnp.where(allowed, jnp.exp2(scores), 0.0).astype(jnp.bfloat16)
            total[head] += jnp.dot(weights, value, preferred_element_type=jnp.float32)

    def needed(plane, row, column):
        behind = here - ((z - plane) * N_Y * N_CORE + row * N_CORE + column)
        return wanted(plane, row, y) & (behind >= 0) & (behind <= WINDOW)

    add_block(0, y, core)
    for plane in (1, 2):

        @pl.when(z >= plane)
        def _():
            along_z(plane).wait_recv()
            share(plane)
            pl.when(wanted(plane, y, y))(to_sibling(plane, y).start)

    @pl.loop(1, 3 * N_Y + 1)
    def _(step):
        plane, back = step // N_Y, step % N_Y
        row = (y + N_Y - back) % N_Y

        @pl.when((step < 3 * N_Y) & wanted(plane, row, y))
        def _():
            @pl.when(back > 0)
            def _():
                slot = place(plane, row, core)
                remote(
                    held.at[slot], held.at[slot], y_sends, y_arrivals, 3 * plane + back - 1,
                    (peer((0, 1, 0)), x),
                ).wait_recv()
                to_sibling(plane, row).start()

            pl.when(needed(plane, row, core))(lambda: add_block(plane, row, core))

        plane, back = (step - 1) // N_Y, (step - 1) % N_Y
        row = (y + N_Y - back) % N_Y

        @pl.when(wanted(plane, row, y))
        def _():
            from_sibling(plane, row).wait_recv()
            pl.when(needed(plane, row, 1 - core))(lambda: add_block(plane, row, 1 - core))

    for head in range(heads):
        out[:, head * HD : (head + 1) * HD] = (
            total[head, :, :HD] / total[head, :, HD:]
        ).astype(out.dtype)
    for plane in (1, 2):
        pl.when(z + plane < N_Z)(along_z(plane).wait_send)
    for plane in (0, 1, 2):
        for step in (1, 2, 3):
            pl.when(wanted(plane, y, (y + step) % N_Y))(along_y(plane, step).wait_send)
        for row in range(N_Y):
            pl.when(wanted(plane, row, y))(to_sibling(plane, row).wait_send)
    for index in (0, 1):
        direct(index).wait_send()
        onward(index).wait_send()


def draft(merged, embed, w_query, w_kv, embed_gain, merged_gain, q_gain, k_gain, cosine, sine, row_start):
    rows, cut = merged.shape
    heads = w_query.shape[1] // HD
    wide = w_query.shape[1] + w_kv.shape[1]
    hbm = pl.BlockSpec(memory_space=pl.ANY)
    vmem = pl.BlockSpec(memory_space=pltpu.VMEM)
    dma = pltpu.SemaphoreType.DMA
    return pl.pallas_call(
        draft_kernel,
        out_shape=jax.ShapeDtypeStruct((rows, heads * HD), jnp.bfloat16),
        in_specs=[hbm] * 4 + [vmem] * 7,
        out_specs=vmem,
        scratch_shapes=[
            pltpu.VMEM((N_X, rows, cut), jnp.bfloat16),
            pltpu.VMEM((rows, D), jnp.bfloat16),
            pltpu.VMEM((rows, D), jnp.bfloat16),
            pltpu.VMEM((rows, wide), jnp.float32),
            pltpu.VMEM((rows, wide), jnp.float32),
            pltpu.VMEM((rows, HD), jnp.float32),
            pltpu.VMEM((heads, rows, HD), jnp.bfloat16),
            pltpu.VMEM((3 * N_Y * N_CORE, 2, rows, HD), jnp.bfloat16),
            pltpu.VMEM((heads, rows, 2 * HD), jnp.float32),
            pltpu.VMEM((2 * D, heads * HD), jnp.bfloat16),
            pltpu.VMEM((2 * D, w_kv.shape[1]), jnp.bfloat16),
            dma((4,)), dma((4,)), dma((2,)), dma((2,)), dma((9,)), dma((9,)), dma((12,)), dma((12,)),
            dma((4,)),
        ],
        compiler_params=pltpu.CompilerParams(
            collective_id=3, has_side_effects=True, vmem_limit_bytes=56 << 20
        ),
        name="draft",
    )(
        merged, embed, w_query, w_kv, embed_gain[None, :], merged_gain[None, :], q_gain[None, :],
        k_gain[None, :], cosine, sine, row_start,
    )


def body(
    tokens,
    low_tap,
    mid_tap,
    next_embed,
    expert_ids,
    gate_weights,
    segments,
    moe_gain,
    w_gate,
    w_up,
    w_down,
    merge_weight,
    embed_gain,
    merged_gain,
    w_query,
    w_kv,
    q_gain,
    k_gain,
):
    rows = tokens.shape[0]
    planes = jnp.arange(N_X, dtype=jnp.int32)
    owners = peer(offset_of(jnp.arange(PEERS, dtype=jnp.int32)))[None, :] * N_X + planes[:, None]
    hits = expert_ids[None, None, :, :] == owners[:, :, None, None]
    member = jnp.any(hits, axis=3)
    share = jnp.sum(jnp.where(hits, gate_weights[None, None], 0.0), axis=3)
    order = jnp.arange(rows, dtype=jnp.int32)
    earlier = (order[:, None] < order[None, :]).astype(jnp.bfloat16)
    ranks = jnp.dot(member.astype(jnp.bfloat16), earlier, preferred_element_type=jnp.float32)
    spots = jnp.where(member, ranks + CAPACITY * lax.axis_index("group"), NOWHERE)
    routing = jnp.stack([spots, share], axis=1)
    merged_part, embed_rows = experts(
        tokens, routing, low_tap, mid_tap, next_embed, w_gate[0], w_up[0], w_down[0],
        merge_weight, moe_gain[None, :],
    )
    block_rows = embed_rows.shape[0]
    first = lax.axis_index("expert") * block_rows
    positions = lax.dynamic_slice_in_dim(segment_positions(segments), first, block_rows)
    row_start = (first + jnp.arange(block_rows, dtype=jnp.int32) - positions)[:, None]
    cosine, sine = rotation(positions)
    return draft(
        merged_part, embed_rows, w_query, w_kv.reshape(w_kv.shape[0], -1), embed_gain, merged_gain,
        q_gain, k_gain, cosine, sine, row_start,
    )


def solution(mesh):
    return jax.shard_map(
        body,
        mesh=mesh,
        in_specs=(
            P(("expert", "group"), None),
            P(("expert", "group"), None),
            P(("expert", "group"), None),
            P(("expert", "group"), None),
            P(("expert", "group"), None),
            P(("expert", "group"), None),
            P(),
            P(),
            P(("expert", "group"), None, None),
            P(("expert", "group"), None, None),
            P(("expert", "group"), None, None),
            P(None, "group"),
            P(),
            P(),
            P(None, "group"),
            P(None, None, "group"),
            P(),
            P(),
        ),
        out_specs=P("expert", "group"),
        check_vma=False,
    )
```

```python
import jax
import jax.numpy as jnp
import numpy as np
from jax import lax
from jax.experimental import pallas as pl
from jax.experimental.pallas import tpu as pltpu
from jax.sharding import PartitionSpec as P

D = 2048
HD = 128
TOPK = 8
SEGS = 4


EPSILON = 1e-06
THETA = 1000000.0
LOG2E = 1.4426950408889634
MESH = pl.DeviceIdType.MESH
N_Z, N_Y, N_CORE, N_X = 4, 4, 2, 4
PEERS = N_Z * N_Y * N_CORE
ROUND = 8
WINDOW = 16
CUTS = 4
HALVES = (0, 1)
CAPACITY = 12
NOWHERE = -1000.0


def offset_of(slot):
    turn = slot // N_CORE
    return ((turn // N_Y + turn) % N_Z, turn % N_Y, slot % N_CORE)


def peer(offset, sign=1):
    here = lax.axis_index("expert")
    z = (here // (N_Y * N_CORE) + sign * offset[0] + N_Z) % N_Z
    y = (here // N_CORE % N_Y + sign * offset[1] + N_Y) % N_Y
    core = (here + offset[2]) % N_CORE
    return (z * N_Y + y) * N_CORE + core


def remote(source, target, sends, arrivals, slot, device):
    return pltpu.make_async_remote_copy(
        src_ref=source,
        dst_ref=target,
        send_sem=sends.at[slot],
        recv_sem=arrivals.at[slot],
        device_id=device,
        device_id_type=MESH,
    )


def greet(devices):
    barrier = pltpu.get_barrier_semaphore()
    for device in devices:
        pl.semaphore_signal(barrier, inc=1, device_id=device, device_id_type=MESH)
    pl.semaphore_wait(barrier, len(devices))


def across(step):
    return (lax.axis_index("expert"), (lax.axis_index("group") + step) % N_X)


def experts_kernel(
    tokens, choices, low, mid, embed, w_gate, w_up, w_down, w_merge, gain, segments, freqs,
    merged, embed_rows, cosine, sine, row_start,
    routing, route, place, weights, shares, all_tokens, packed, arrived, normed, hidden, returned,
    total, partial, halves, high, low_rows, mid_rows, merge_total,
    gate_mat, up_mat, down_mat, merge_mat,
    own, route_sends, route_arrivals, token_sends, token_arrivals, out_sends, out_arrivals,
    back_sends, back_arrivals, tap_sends, tap_arrivals, sum_sends, sum_arrivals,
    high_sends, high_arrivals,
):
    x = lax.axis_index("group")
    rows = tokens.shape[0]
    slots = CAPACITY * N_X
    batch = ROUND * slots
    batches = PEERS // ROUND
    cut = D // CUTS
    steps = range(1, N_X)
    mine = pl.ds(pl.multiple_of(x * rows, rows), rows)

    def columns(part):
        return pl.ds(pl.multiple_of(part * cut, cut), cut)

    def slot_rows(slot):
        return pl.ds(pl.multiple_of(slot * slots, slots), slots)

    def batch_rows(index):
        return pl.ds(pl.multiple_of(index * batch, batch), batch)

    kept = [
        pltpu.make_async_copy(source, target, own.at[index])
        for index, (source, target) in enumerate(
            (
                (tokens, all_tokens.at[mine]),
                (w_gate, gate_mat),
                (w_up, up_mat),
                (w_down, down_mat),
                (low, low_rows.at[mine]),
                (mid, mid_rows.at[mine]),
                (w_merge, merge_mat),
                (embed, embed_rows.at[mine]),
            )
        )
    ]
    for copy in kept:
        copy.start()

    barrier = pltpu.get_barrier_semaphore()
    for step in steps:
        pl.semaphore_signal(barrier, inc=1, device_id=across(step), device_id_type=MESH)

    @pl.loop(1, PEERS)
    def _(slot):
        pl.semaphore_signal(
            barrier, inc=1, device_id=(peer(offset_of(slot), -1), x), device_id_type=MESH
        )

    slot = lax.broadcasted_iota(jnp.int32, (PEERS, 1), 0)
    owner = (peer(offset_of(slot)) * N_X).astype(jnp.float32)
    earlier = lax.broadcasted_iota(jnp.int32, (rows, rows), 0) < lax.broadcasted_iota(
        jnp.int32, (rows, rows), 1
    )
    earlier = jnp.where(earlier, 1.0, 0.0).astype(jnp.bfloat16)
    for plane in range(N_X):
        member = jnp.zeros((PEERS, rows), jnp.float32)
        share = jnp.zeros((PEERS, rows), jnp.float32)
        for choice in range(TOPK):
            hit = choices[choice : choice + 1, :] == owner + plane
            member += jnp.where(hit, 1.0, 0.0)
            share += jnp.where(hit, choices[TOPK + choice : TOPK + choice + 1, :], 0.0)
        ranks = jnp.dot(member.astype(jnp.bfloat16), earlier, preferred_element_type=jnp.float32)
        shift = (CAPACITY * x).astype(jnp.float32)
        routing[plane, 0] = jnp.where(member > 0.0, ranks + shift, NOWHERE)
        routing[plane, 1] = share

    pl.semaphore_wait(barrier, PEERS - 1 + N_X - 1)

    def route_copy(step):
        return remote(
            routing.at[(x + step) % N_X], route.at[x], route_sends, route_arrivals, step - 1,
            across(step),
        )

    def token_copy(part, step):
        return remote(
            tokens.at[:, columns(part)], all_tokens.at[mine, columns(part)],
            token_sends, token_arrivals, (N_X - 1) * part + step - 1, across(step),
        )

    def outward(slot, part):
        return remote(
            packed.at[slot_rows(slot), columns(part)], arrived.at[slot_rows(slot), columns(part)],
            out_sends, out_arrivals, PEERS * part + slot, (peer(offset_of(slot)), x),
        )

    def homeward(slot, part):
        return remote(
            packed.at[slot_rows(slot), columns(part)], returned.at[slot_rows(slot), columns(part)],
            back_sends, back_arrivals, PEERS * part + slot, (peer(offset_of(slot), -1), x),
        )

    def tap_copy(index, step):
        source = (low, mid, embed)[index]
        target = (low_rows, mid_rows, embed_rows)[index]
        return remote(
            source, target.at[mine], tap_sends, tap_arrivals, (N_X - 1) * index + step - 1,
            across(step),
        )

    def sum_copy(part, step):
        theirs = pl.ds(pl.multiple_of((x + step) % N_X * rows, rows), rows)
        return remote(
            partial.at[theirs, columns(part)], halves.at[step - 1, :, columns(part)],
            sum_sends, sum_arrivals, (N_X - 1) * part + step - 1, across(step),
        )

    def high_copy(part, step):
        return remote(
            high.at[mine, columns(part)], high.at[mine, columns(part)],
            high_sends, high_arrivals, (N_X - 1) * part + step - 1, across(step),
        )

    for step in steps:
        route_copy(step).start()
    for part in range(CUTS):
        for step in steps:
            token_copy(part, step).start()
    route[x] = routing[x]
    for step in steps:
        route_copy(step).wait_recv()

    def spread_line(kind, slot):
        return jnp.concatenate(
            [route[block, kind, pl.ds(slot, 1), :] for block in range(N_X)], axis=1
        )

    def match(slot):
        lines = lax.broadcasted_iota(jnp.int32, (slots, N_X * rows), 0).astype(jnp.float32)
        return lines == spread_line(0, slot)

    @pl.loop(0, PEERS)
    def _(slot):
        place[slot_rows(slot), :] = jnp.where(match(slot), 1.0, 0.0).astype(jnp.bfloat16)

    kept[0].wait()

    @pl.loop(0, CUTS)
    def _(part):
        for step in steps:
            token_copy(part, step).wait_recv()

        @pl.loop(0, batches)
        def _(index):
            span = batch_rows(index)
            packed[span, columns(part)] = jnp.dot(
                place[span, :], all_tokens[:, columns(part)], preferred_element_type=jnp.float32
            ).astype(jnp.bfloat16)

            @pl.loop(index * ROUND, (index + 1) * ROUND)
            def _(slot):
                pl.when(slot > 0)(lambda: outward(slot, part).start())

        arrived[slot_rows(0), columns(part)] = packed[slot_rows(0), columns(part)]

    for index in range(3):
        for step in steps:
            tap_copy(index, step).start()

    @pl.loop(0, batches)
    def _(index):
        @pl.loop(0, ROUND)
        def _(inner):
            slot = index * ROUND + inner
            weights[slot_rows(inner), :] = jnp.where(match(slot), spread_line(1, slot), 0.0)

        shares[:, batch_rows(index)] = weights[...].T.astype(jnp.bfloat16)

    line = lax.axis_index("expert") * N_X * rows + lax.broadcasted_iota(
        jnp.int32, (N_X * rows, 1), 0
    )
    line = line.astype(jnp.float32)
    start = jnp.zeros_like(line)
    for label in range(1, SEGS):
        below = jnp.where(segments[...] < label, 1.0, 0.0)
        count = jnp.sum(jnp.sum(below, axis=1, keepdims=True), axis=0, keepdims=True)
        start = jnp.maximum(start, jnp.where(count <= line, count, 0.0))
    row_start[...] = start.astype(jnp.int32)
    angles = (line - start) * freqs[...]
    signs = jnp.where(lax.broadcasted_iota(jnp.int32, (1, HD), 1) < HD // 2, -1.0, 1.0)
    cosine[...] = jnp.cos(angles)
    sine[...] = jnp.sin(angles) * signs
    for copy in kept[1:]:
        copy.wait()

    def reply(index, part):
        span = batch_rows(index)
        packed[span, columns(part)] = jnp.dot(
            hidden[span, :], down_mat[:, columns(part)], preferred_element_type=jnp.float32
        ).astype(jnp.bfloat16)

        @pl.loop(index * ROUND, (index + 1) * ROUND)
        def _(slot):
            pl.when(slot > 0)(lambda: homeward(slot, part).start())

        @pl.when(index == 0)
        def _():
            returned[slot_rows(0), columns(part)] = packed[slot_rows(0), columns(part)]

    def each_copy(index, act):
        @pl.loop(0, ROUND * CUTS)
        def _(inner):
            slot = index * ROUND + inner % ROUND
            pl.when(slot > 0)(lambda: act(slot, inner // ROUND))

    @pl.loop(0, batches)
    def _(index):
        each_copy(index, lambda slot, part: outward(slot, part).wait_recv())

        @pl.loop(0, ROUND)
        def _(inner):
            values = arrived[slot_rows(index * ROUND + inner), :].astype(jnp.float32)
            size = lax.rsqrt(jnp.mean(values * values, axis=-1, keepdims=True) + EPSILON)
            normed[slot_rows(inner), :] = (values * size * gain[...]).astype(jnp.bfloat16)

        @pl.loop(0, w_gate.shape[1] // 256)
        def _(tile):
            tiles = pl.ds(pl.multiple_of(tile * 256, 256), 256)
            gate = jnp.dot(normed[...], gate_mat[:, tiles], preferred_element_type=jnp.float32)
            up = jnp.dot(normed[...], up_mat[:, tiles], preferred_element_type=jnp.float32)
            hidden[batch_rows(index), tiles] = (gate / (1.0 + jnp.exp(-gate)) * up).astype(
                jnp.bfloat16
            )

        each_copy(index, lambda slot, part: outward(slot, part).wait_send())
        reply(index, 0)

    @pl.loop(batches, CUTS * batches)
    def _(turn):
        reply(turn % batches, turn // batches)

    for index in range(2):
        for step in steps:
            tap_copy(index, step).wait_recv()
    merge_total[...] = jnp.zeros_like(merge_total)

    def add_merge(source, index, part):
        depth = pl.ds(pl.multiple_of(index * D + part * cut, cut), cut)
        merge_total[...] += jnp.dot(
            source[:, columns(part)], merge_mat[depth, :], preferred_element_type=jnp.float32
        )

    @pl.loop(0, CUTS)
    def _(part):
        add_merge(low_rows, 0, part)
        add_merge(mid_rows, 1, part)

    def add_high(part):
        for step in steps:
            high_copy(part, step).wait_recv()
        add_merge(high, 2, part)

    @pl.loop(0, CUTS)
    def _(part):
        total[...] = jnp.zeros_like(total)

        @pl.loop(0, batches)
        def _(index):
            @pl.loop(index * ROUND, (index + 1) * ROUND)
            def _(slot):
                pl.when(slot > 0)(lambda: homeward(slot, part).wait_recv())

            span = batch_rows(index)
            total[...] += jnp.dot(
                shares[:, span], returned[span, columns(part)], preferred_element_type=jnp.float32
            )

        partial[:, columns(part)] = total[...].astype(jnp.bfloat16)
        for step in steps:
            sum_copy(part, step).start()
        mixed = all_tokens[mine, columns(part)].astype(jnp.float32) + total[mine, :]
        for step in steps:
            sum_copy(part, step).wait_recv()
            mixed += halves[step - 1, :, columns(part)].astype(jnp.float32)
        high[mine, columns(part)] = mixed.astype(jnp.bfloat16)
        for step in steps:
            high_copy(part, step).start()
        pl.when(part > 0)(lambda: add_high(part - 1))

    add_high(CUTS - 1)
    merged[...] = merge_total[...].astype(jnp.bfloat16)

    @pl.loop(0, batches)
    def _(index):
        each_copy(index, lambda slot, part: homeward(slot, part).wait_send())

    for step in steps:
        route_copy(step).wait_send()
        tap_copy(2, step).wait_recv()
        for index in range(3):
            tap_copy(index, step).wait_send()

        @pl.loop(0, CUTS)
        def _(part):
            token_copy(part, step).wait_send()
            sum_copy(part, step).wait_send()
            high_copy(part, step).wait_send()


def experts(
    tokens, choices, low, mid, embed, w_gate, w_up, w_down, w_merge, gain, segments, freqs
):
    rows, width, out_width = tokens.shape[0], w_gate.shape[1], w_merge.shape[1]
    everyone = N_X * rows
    slots = CAPACITY * N_X
    hbm = pl.BlockSpec(memory_space=pl.ANY)
    vmem = pl.BlockSpec(memory_space=pltpu.VMEM)
    dma = pltpu.SemaphoreType.DMA

    def half(*shape):
        return pltpu.VMEM(shape, jnp.bfloat16)

    def full(*shape):
        return pltpu.VMEM(shape, jnp.float32)

    few, many = (N_X - 1) * CUTS, PEERS * CUTS
    return pl.pallas_call(
        experts_kernel,
        out_shape=(
            jax.ShapeDtypeStruct((everyone, out_width), jnp.bfloat16),
            jax.ShapeDtypeStruct((everyone, D), jnp.bfloat16),
            jax.ShapeDtypeStruct((everyone, HD), jnp.float32),
            jax.ShapeDtypeStruct((everyone, HD), jnp.float32),
            jax.ShapeDtypeStruct((everyone, 1), jnp.int32),
        ),
        in_specs=[hbm, vmem] + [hbm] * 7 + [vmem] * 3,
        out_specs=(vmem, hbm, vmem, vmem, vmem),
        scratch_shapes=[
            full(N_X, 2, PEERS, rows),
            full(N_X, 2, PEERS, rows),
            half(PEERS * slots, everyone),
            full(ROUND * slots, everyone),
            half(everyone, PEERS * slots),
            half(everyone, D),
            half(PEERS * slots, D),
            half(PEERS * slots, D),
            half(ROUND * slots, D),
            half(PEERS * slots, width),
            half(PEERS * slots, D),
            full(everyone, D // CUTS),
            half(everyone, D),
            half(N_X - 1, rows, D),
            half(everyone, D),
            half(everyone, D),
            half(everyone, D),
            full(everyone, out_width),
            half(D, width),
            half(D, width),
            half(width, D),
            half(3 * D, out_width),
            dma((9,)),
            dma((N_X - 1,)), dma((N_X - 1,)),
            dma((few,)), dma((few,)),
            dma((many,)), dma((many,)),
            dma((many,)), dma((many,)),
            dma((9,)), dma((9,)),
            dma((few,)), dma((few,)),
            dma((few,)), dma((few,)),
        ],
        compiler_params=pltpu.CompilerParams(
            collective_id=2, has_side_effects=True, vmem_limit_bytes=60 << 20
        ),
        cost_estimate=pl.CostEstimate(
            flops=6 * PEERS * slots * D * width, bytes_accessed=40 << 20, transcendentals=0
        ),
        name="experts",
    )(
        tokens, choices, low, mid, embed, w_gate, w_up, w_down, w_merge, gain, segments, freqs
    )


def draft_kernel(
    merged, embed, w_query, w_kv, embed_gain, merged_gain, q_gain, k_gain, cosine, sine, row_start,
    out,
    pieces, embeds, joined, embed_total, merged_total, squares, query, held, total,
    query_mat, kv_mat,
    x_sends, x_arrivals, z_sends, z_arrivals, y_sends, y_arrivals, core_sends, core_arrivals, own,
):
    rows, cut = merged.shape
    heads = query.shape[0]
    here, x = lax.axis_index("expert"), lax.axis_index("group")
    z, y, core = here // (N_Y * N_CORE), here // N_CORE % N_Y, here % N_CORE
    loads = [
        pltpu.make_async_copy(source, target, own.at[index])
        for index, (source, target) in enumerate(
            ((merged, pieces.at[x]), (embed, embeds), (w_query, query_mat), (w_kv, kv_mat))
        )
    ]
    for load in loads:
        load.start()
    greet(
        [across(step) for step in (1, 2, 3)]
        + [(peer((step, 0, 0)), x) for step in (1, 2, 3)]
        + [(peer((0, step, 0)), x) for step in (1, 2, 3)]
        + [(peer((0, 0, 1)), x)]
    )
    near, far = 1, N_X - 1
    size = rows // len(HALVES)

    def span_of(half):
        return pl.ds(half * size, size)

    def direct(index, half):
        span = span_of(half)
        return remote(
            merged.at[span], pieces.at[x, span], x_sends, x_arrivals, 4 * half + index,
            across((near, far)[index]),
        )

    def onward(index, half):
        block = (x + (far, near)[index]) % N_X
        span = pl.ds(half * size + index * size // 2, size // 2)
        return remote(
            pieces.at[block, span], pieces.at[block, span], x_sends, x_arrivals,
            4 * half + 2 + index, across((near, far)[index]),
        )

    for half in HALVES:
        for index in (0, 1):
            direct(index, half).start()

    def add_part(source, depth, target):
        target[:, : heads * HD] += jnp.dot(
            source, query_mat[depth, :], preferred_element_type=jnp.float32
        )
        target[:, heads * HD :] += jnp.dot(
            source, kv_mat[depth, :], preferred_element_type=jnp.float32
        )

    def columns(part):
        return pl.ds(pl.multiple_of(part * cut, cut), cut)

    embed_total[...] = jnp.zeros_like(embed_total)
    merged_total[...] = jnp.zeros_like(merged_total)
    squares[...] = jnp.zeros_like(squares)
    loads[1].wait()
    chunk = rows // 8

    @pl.loop(0, 8)
    def _(index):
        span = pl.ds(pl.multiple_of(index * chunk, chunk), chunk)
        values = embeds[span, :].astype(jnp.float32)
        size = lax.rsqrt(jnp.mean(values * values, axis=-1, keepdims=True) + EPSILON)
        joined[span, :] = (values * size * embed_gain[...]).astype(jnp.bfloat16)

    for load in (loads[0], loads[2], loads[3]):
        load.wait()

    @pl.loop(0, N_X)
    def _(part):
        add_part(joined[:, columns(part)], columns(part), embed_total)

    def pass_on(half):
        for index in (0, 1):
            direct(index, half).wait_recv()
            onward(index, half).start()

    def add_piece(block, half):
        span = span_of(half)
        values = pieces[block, span].astype(jnp.float32)
        squares[span, :] += jnp.broadcast_to(
            jnp.sum(values * values, axis=-1, keepdims=True), (size, HD)
        )
        source = (values * merged_gain[:, columns(block)]).astype(jnp.bfloat16)
        joined[span, columns(block)] = source
        depth = pl.ds(pl.multiple_of(D + block * cut, cut), cut)
        merged_total[span, heads * HD :] += jnp.dot(
            source, kv_mat[depth, :], preferred_element_type=jnp.float32
        )

    def project(index, span):
        shrink = lax.rsqrt(squares[span, :1] * (1.0 / D) + EPSILON)
        lanes = slice(index * HD, (index + 1) * HD)
        return embed_total[span, lanes] + merged_total[span, lanes] * shrink

    def turned(values, gain, span):
        scale = lax.rsqrt(jnp.mean(values * values, axis=-1, keepdims=True) + EPSILON)
        values = values * scale * gain[...]
        return values * cosine[span, :] + pltpu.roll(values, HD // 2, 1) * sine[span, :]

    def place(plane, row, column):
        return (plane * N_Y + row) * N_CORE + column

    def wanted(plane, row, reader):
        near = (plane == 0) & (row <= reader)
        return near | ((plane == 1) & (z >= 1)) | ((plane == 2) & (z >= 2) & (row >= reader))

    def along_z(plane, half):
        span = span_of(half)
        return remote(
            held.at[place(0, y, core), :, span], held.at[place(plane, y, core), :, span],
            z_sends, z_arrivals, 2 * (plane - 1) + half, (peer((plane, 0, 0)), x),
        )

    def along_y(plane, step, half):
        part = held.at[place(plane, y, core), :, span_of(half)]
        return remote(
            part, part, y_sends, y_arrivals, 2 * (3 * plane + step - 1) + half,
            (peer((0, step, 0)), x),
        )

    def from_y(plane, step, row, half):
        part = held.at[place(plane, row, core), :, span_of(half)]
        return remote(
            part, part, y_sends, y_arrivals, 2 * (3 * plane + step - 1) + half,
            (peer((0, 1, 0)), x),
        )

    def sibling(plane, row, column, half):
        part = held.at[place(plane, row, column), :, span_of(half)]
        return remote(
            part, part, core_sends, core_arrivals, 2 * (N_Y * plane + row) + half,
            (peer((0, 0, 1)), x),
        )

    def share(plane, half):
        for step in (1, 2, 3):
            pl.when(wanted(plane, y, (y + step) % N_Y))(along_y(plane, step, half).start)

    total[...] = jnp.zeros_like(total)
    pass_on(0)
    for half in HALVES:
        for turn in (0, 3, 1):
            add_piece((x + turn) % N_X, half)
        if half == 0:
            pass_on(1)
        for index in (0, 1):
            onward(index, half).wait_recv()
        add_piece((x + 2) % N_X, half)
        span = span_of(half)
        mine = place(0, y, core)
        held[mine, 0, span] = turned(project(heads, span), k_gain, span).astype(jnp.bfloat16)
        held[mine, 1, span] = project(heads + 1, span).astype(jnp.bfloat16)
        for plane in (2, 1):
            pl.when(z + plane < N_Z)(along_z(plane, half).start)
        share(0, half)
        sibling(0, y, core, half).start()

    @pl.loop(0, N_X)
    def _(part):
        depth = pl.ds(pl.multiple_of(D + part * cut, cut), cut)
        merged_total[:, : heads * HD] += jnp.dot(
            joined[:, columns(part)], query_mat[depth, :], preferred_element_type=jnp.float32
        )

    everything = pl.ds(0, rows)
    for index in range(heads):
        query[index] = (
            turned(project(index, everything), q_gain, everything) * (HD**-0.5 * LOG2E)
        ).astype(jnp.bfloat16)

    def add_block(plane, row, column):
        slot = place(plane, row, column)
        first = ((z - plane) * N_Y * N_CORE + row * N_CORE + column) * rows
        key = held[slot, 0]
        value = jnp.concatenate([held[slot, 1], jnp.ones((rows, HD), jnp.bfloat16)], axis=1)
        query_index = here * rows + lax.broadcasted_iota(jnp.int32, (rows, rows), 0)
        key_index = first + lax.broadcasted_iota(jnp.int32, (rows, rows), 1)
        allowed = (key_index <= query_index) & (key_index >= row_start[...])
        for head in range(heads):
            scores = lax.dot_general(
                query[head], key, (((1,), (1,)), ((), ())), preferred_element_type=jnp.float32
            )
            weights = jnp.where(allowed, jnp.exp2(scores), 0.0).astype(jnp.bfloat16)
            total[head] += jnp.dot(weights, value, preferred_element_type=jnp.float32)

    def needed(plane, row, column):
        behind = here - ((z - plane) * N_Y * N_CORE + row * N_CORE + column)
        return wanted(plane, row, y) & (behind >= 0) & (behind <= WINDOW)

    def pass_plane(plane, half):
        @pl.when(z >= plane)
        def _():
            along_z(plane, half).wait_recv()
            share(plane, half)
            pl.when(wanted(plane, y, y))(sibling(plane, y, core, half).start)

    for half in HALVES:
        pass_plane(1, half)
    add_block(0, y, core)
    for half in HALVES:
        pass_plane(2, half)

    @pl.loop(1, 3 * N_Y + 1)
    def _(step):
        plane, back = step // N_Y, step % N_Y
        row = (y + N_Y - back) % N_Y

        @pl.when((step < 3 * N_Y) & wanted(plane, row, y))
        def _():
            @pl.when(back > 0)
            def _():
                for half in HALVES:
                    from_y(plane, back, row, half).wait_recv()
                    sibling(plane, row, core, half).start()

            pl.when(needed(plane, row, core))(lambda: add_block(plane, row, core))

        plane, back = (step - 1) // N_Y, (step - 1) % N_Y
        row = (y + N_Y - back) % N_Y

        @pl.when(wanted(plane, row, y))
        def _():
            for half in HALVES:
                sibling(plane, row, 1 - core, half).wait_recv()
            pl.when(needed(plane, row, 1 - core))(lambda: add_block(plane, row, 1 - core))

    for head in range(heads):
        out[:, head * HD : (head + 1) * HD] = (
            total[head, :, :HD] / total[head, :, HD:]
        ).astype(out.dtype)
    for half in HALVES:
        for plane in (1, 2):
            pl.when(z + plane < N_Z)(along_z(plane, half).wait_send)
        for plane in (0, 1, 2):
            for step in (1, 2, 3):
                pl.when(wanted(plane, y, (y + step) % N_Y))(along_y(plane, step, half).wait_send)
            for row in range(N_Y):
                pl.when(wanted(plane, row, y))(sibling(plane, row, core, half).wait_send)
        for index in (0, 1):
            direct(index, half).wait_send()
            onward(index, half).wait_send()


def draft(merged, embed, w_query, w_kv, embed_gain, merged_gain, q_gain, k_gain, cosine, sine, row_start):
    rows, cut = merged.shape
    heads = w_query.shape[1] // HD
    wide = w_query.shape[1] + w_kv.shape[1]
    hbm = pl.BlockSpec(memory_space=pl.ANY)
    vmem = pl.BlockSpec(memory_space=pltpu.VMEM)
    dma = pltpu.SemaphoreType.DMA
    return pl.pallas_call(
        draft_kernel,
        out_shape=jax.ShapeDtypeStruct((rows, heads * HD), jnp.bfloat16),
        in_specs=[hbm] * 4 + [vmem] * 7,
        out_specs=vmem,
        scratch_shapes=[
            pltpu.VMEM((N_X, rows, cut), jnp.bfloat16),
            pltpu.VMEM((rows, D), jnp.bfloat16),
            pltpu.VMEM((rows, D), jnp.bfloat16),
            pltpu.VMEM((rows, wide), jnp.float32),
            pltpu.VMEM((rows, wide), jnp.float32),
            pltpu.VMEM((rows, HD), jnp.float32),
            pltpu.VMEM((heads, rows, HD), jnp.bfloat16),
            pltpu.VMEM((3 * N_Y * N_CORE, 2, rows, HD), jnp.bfloat16),
            pltpu.VMEM((heads, rows, 2 * HD), jnp.float32),
            pltpu.VMEM((2 * D, heads * HD), jnp.bfloat16),
            pltpu.VMEM((2 * D, w_kv.shape[1]), jnp.bfloat16),
            dma((8,)), dma((8,)), dma((4,)), dma((4,)), dma((18,)), dma((18,)), dma((24,)), dma((24,)),
            dma((4,)),
        ],
        compiler_params=pltpu.CompilerParams(
            collective_id=3, has_side_effects=True, vmem_limit_bytes=56 << 20
        ),
        name="draft",
    )(
        merged, embed, w_query, w_kv, embed_gain[None, :], merged_gain[None, :], q_gain[None, :],
        k_gain[None, :], cosine, sine, row_start,
    )


def body(
    tokens,
    low_tap,
    mid_tap,
    next_embed,
    expert_ids,
    gate_weights,
    segments,
    moe_gain,
    w_gate,
    w_up,
    w_down,
    merge_weight,
    embed_gain,
    merged_gain,
    w_query,
    w_kv,
    q_gain,
    k_gain,
):
    choices = jnp.concatenate([expert_ids.astype(jnp.float32), gate_weights], axis=1).T
    half = HD // 2
    freqs = np.power(THETA, -np.arange(half) * 2.0 / HD).astype(np.float32)
    freqs = np.concatenate([freqs, freqs])[None, :]
    merged, embed_rows, cosine, sine, row_start = experts(
        tokens, choices, low_tap, mid_tap, next_embed, w_gate[0], w_up[0], w_down[0],
        merge_weight, moe_gain[None, :], segments.reshape(-1, HD), jnp.asarray(freqs),
    )
    return draft(
        merged, embed_rows, w_query, w_kv.reshape(w_kv.shape[0], -1), embed_gain, merged_gain,
        q_gain, k_gain, cosine, sine, row_start,
    )


def solution(mesh):
    return jax.shard_map(
        body,
        mesh=mesh,
        in_specs=(
            P(("expert", "group"), None),
            P(("expert", "group"), None),
            P(("expert", "group"), None),
            P(("expert", "group"), None),
            P(("expert", "group"), None),
            P(("expert", "group"), None),
            P(),
            P(),
            P(("expert", "group"), None, None),
            P(("expert", "group"), None, None),
            P(("expert", "group"), None, None),
            P(None, "group"),
            P(),
            P(),
            P(None, "group"),
            P(None, None, "group"),
            P(),
            P(),
        ),
        out_specs=P("expert", "group"),
        check_vma=False,
    )
```

```python
import jax
import jax.numpy as jnp
import numpy as np
from jax import lax
from jax.experimental import pallas as pl
from jax.experimental.pallas import tpu as pltpu
from jax.sharding import PartitionSpec as P

D = 2048
HD = 128
TOPK = 8
SEGS = 4


EPSILON = 1e-06
THETA = 1000000.0
LOG2E = 1.4426950408889634
MESH = pl.DeviceIdType.MESH
N_Z, N_Y, N_CORE, N_X = 4, 4, 2, 4
PEERS = N_Z * N_Y * N_CORE
ROUND = 8
WINDOW = 16
CUTS = 4
HALVES = (0, 1)
CAPACITY = 12
NOWHERE = -1000.0


def offset_of(slot):
    turn = slot // N_CORE
    return ((turn // N_Y + turn) % N_Z, turn % N_Y, slot % N_CORE)


def peer(offset, sign=1):
    here = lax.axis_index("expert")
    z = (here // (N_Y * N_CORE) + sign * offset[0] + N_Z) % N_Z
    y = (here // N_CORE % N_Y + sign * offset[1] + N_Y) % N_Y
    core = (here + offset[2]) % N_CORE
    return (z * N_Y + y) * N_CORE + core


def remote(source, target, sends, arrivals, slot, device):
    return pltpu.make_async_remote_copy(
        src_ref=source,
        dst_ref=target,
        send_sem=sends.at[slot],
        recv_sem=arrivals.at[slot],
        device_id=device,
        device_id_type=MESH,
    )


def greet(devices):
    barrier = pltpu.get_barrier_semaphore()
    for device in devices:
        pl.semaphore_signal(barrier, inc=1, device_id=device, device_id_type=MESH)
    pl.semaphore_wait(barrier, len(devices))


def across(step):
    return (lax.axis_index("expert"), (lax.axis_index("group") + step) % N_X)


def experts_kernel(
    tokens, choices, gates, low, mid, embed, w_gate, w_up, w_down, w_merge, gain, segments, freqs,
    merged, embed_rows, cosine, sine, row_start,
    routing, route, place, weights, shares, all_tokens, packed, arrived, normed, hidden, returned,
    total, partial, halves, high, low_rows, mid_rows, merge_total,
    gate_mat, up_mat, down_mat, merge_mat,
    own, route_sends, route_arrivals, token_sends, token_arrivals, out_sends, out_arrivals,
    back_sends, back_arrivals, tap_sends, tap_arrivals, sum_sends, sum_arrivals,
    high_sends, high_arrivals,
):
    x = lax.axis_index("group")
    rows = tokens.shape[0]
    slots = CAPACITY * N_X
    batch = ROUND * slots
    batches = PEERS // ROUND
    cut = D // CUTS
    steps = range(1, N_X)
    mine = pl.ds(pl.multiple_of(x * rows, rows), rows)

    def columns(part):
        return pl.ds(pl.multiple_of(part * cut, cut), cut)

    def slot_rows(slot):
        return pl.ds(pl.multiple_of(slot * slots, slots), slots)

    def batch_rows(index):
        return pl.ds(pl.multiple_of(index * batch, batch), batch)

    kept = [
        pltpu.make_async_copy(source, target, own.at[index])
        for index, (source, target) in enumerate(
            (
                (tokens, all_tokens.at[mine]),
                (w_gate, gate_mat),
                (w_up, up_mat),
                (w_down, down_mat),
                (low, low_rows.at[mine]),
                (mid, mid_rows.at[mine]),
                (w_merge, merge_mat),
                (embed, embed_rows.at[mine]),
            )
        )
    ]
    for copy in kept:
        copy.start()

    barrier = pltpu.get_barrier_semaphore()
    for step in steps:
        pl.semaphore_signal(barrier, inc=1, device_id=across(step), device_id_type=MESH)

    @pl.loop(1, PEERS)
    def _(slot):
        pl.semaphore_signal(
            barrier, inc=1, device_id=(peer(offset_of(slot), -1), x), device_id_type=MESH
        )

    slot = lax.broadcasted_iota(jnp.int32, (PEERS, 1), 0)
    owner = peer(offset_of(slot)) * N_X
    earlier = lax.broadcasted_iota(jnp.int32, (rows, rows), 0) < lax.broadcasted_iota(
        jnp.int32, (rows, rows), 1
    )
    earlier = jnp.where(earlier, 1.0, 0.0).astype(jnp.bfloat16)
    for plane in range(N_X):
        member = jnp.zeros((PEERS, rows), jnp.float32)
        share = jnp.zeros((PEERS, rows), jnp.float32)
        for choice in range(TOPK):
            hit = choices[choice : choice + 1, :] == owner + plane
            member += jnp.where(hit, 1.0, 0.0)
            share += jnp.where(hit, gates[choice : choice + 1, :], 0.0)
        ranks = jnp.dot(member.astype(jnp.bfloat16), earlier, preferred_element_type=jnp.float32)
        shift = (CAPACITY * x).astype(jnp.float32)
        routing[plane, 0] = jnp.where(member > 0.0, ranks + shift, NOWHERE)
        routing[plane, 1] = share

    pl.semaphore_wait(barrier, PEERS - 1 + N_X - 1)

    def route_copy(step):
        return remote(
            routing.at[(x + step) % N_X], route.at[x], route_sends, route_arrivals, step - 1,
            across(step),
        )

    def token_copy(part, step):
        return remote(
            tokens.at[:, columns(part)], all_tokens.at[mine, columns(part)],
            token_sends, token_arrivals, (N_X - 1) * part + step - 1, across(step),
        )

    def outward(slot, part):
        return remote(
            packed.at[slot_rows(slot), columns(part)], arrived.at[slot_rows(slot), columns(part)],
            out_sends, out_arrivals, PEERS * part + slot, (peer(offset_of(slot)), x),
        )

    def homeward(slot, part):
        return remote(
            packed.at[slot_rows(slot), columns(part)], returned.at[slot_rows(slot), columns(part)],
            back_sends, back_arrivals, PEERS * part + slot, (peer(offset_of(slot), -1), x),
        )

    def tap_copy(index, step):
        source = (low, mid, embed)[index]
        target = (low_rows, mid_rows, embed_rows)[index]
        return remote(
            source, target.at[mine], tap_sends, tap_arrivals, (N_X - 1) * index + step - 1,
            across(step),
        )

    def sum_copy(part, step):
        theirs = pl.ds(pl.multiple_of((x + step) % N_X * rows, rows), rows)
        return remote(
            partial.at[theirs, columns(part)], halves.at[step - 1, :, columns(part)],
            sum_sends, sum_arrivals, (N_X - 1) * part + step - 1, across(step),
        )

    def high_copy(part, step):
        return remote(
            high.at[mine, columns(part)], high.at[mine, columns(part)],
            high_sends, high_arrivals, (N_X - 1) * part + step - 1, across(step),
        )

    for step in steps:
        route_copy(step).start()
    for part in range(2):
        for step in steps:
            token_copy(part, step).start()
    route[x] = routing[x]
    for step in steps:
        route_copy(step).wait_recv()

    def spread_line(kind, slot):
        return jnp.concatenate(
            [route[block, kind, pl.ds(slot, 1), :] for block in range(N_X)], axis=1
        )

    def match(slot):
        lines = lax.broadcasted_iota(jnp.int32, (slots, N_X * rows), 0).astype(jnp.float32)
        return lines == spread_line(0, slot)

    @pl.loop(0, PEERS)
    def _(slot):
        place[slot_rows(slot), :] = jnp.where(match(slot), 1.0, 0.0).astype(jnp.bfloat16)

    kept[0].wait()

    @pl.loop(0, CUTS)
    def _(part):
        for step in steps:
            token_copy(part, step).wait_recv()

        @pl.when(part + 2 < CUTS)
        def _():
            for step in steps:
                token_copy(part + 2, step).start()

        @pl.loop(0, batches)
        def _(index):
            span = batch_rows(index)
            packed[span, columns(part)] = jnp.dot(
                place[span, :], all_tokens[:, columns(part)], preferred_element_type=jnp.float32
            ).astype(jnp.bfloat16)

            @pl.loop(index * ROUND, (index + 1) * ROUND)
            def _(slot):
                pl.when(slot > 0)(lambda: outward(slot, part).start())

        arrived[slot_rows(0), columns(part)] = packed[slot_rows(0), columns(part)]

    for index in range(3):
        for step in steps:
            tap_copy(index, step).start()

    @pl.loop(0, batches)
    def _(index):
        @pl.loop(0, ROUND)
        def _(inner):
            slot = index * ROUND + inner
            weights[slot_rows(inner), :] = jnp.where(match(slot), spread_line(1, slot), 0.0)

        shares[:, batch_rows(index)] = weights[...].T.astype(jnp.bfloat16)

    line = lax.axis_index("expert") * N_X * rows + lax.broadcasted_iota(
        jnp.int32, (N_X * rows, 1), 0
    )
    line = line.astype(jnp.float32)
    start = jnp.zeros_like(line)
    for label in range(1, SEGS):
        below = jnp.where(segments[...] < label, 1.0, 0.0)
        count = jnp.sum(jnp.sum(below, axis=1, keepdims=True), axis=0, keepdims=True)
        start = jnp.maximum(start, jnp.where(count <= line, count, 0.0))
    row_start[...] = start.astype(jnp.int32)
    angles = (line - start) * freqs[...]
    signs = jnp.where(lax.broadcasted_iota(jnp.int32, (1, HD), 1) < HD // 2, -1.0, 1.0)
    cosine[...] = jnp.cos(angles)
    sine[...] = jnp.sin(angles) * signs
    for copy in kept[1:]:
        copy.wait()

    def reply(index, part):
        span = batch_rows(index)
        packed[span, columns(part)] = jnp.dot(
            hidden[span, :], down_mat[:, columns(part)], preferred_element_type=jnp.float32
        ).astype(jnp.bfloat16)

        @pl.loop(index * ROUND, (index + 1) * ROUND)
        def _(slot):
            pl.when(slot > 0)(lambda: homeward(slot, part).start())

        @pl.when(index == 0)
        def _():
            returned[slot_rows(0), columns(part)] = packed[slot_rows(0), columns(part)]

    def each_copy(index, act):
        @pl.loop(0, ROUND * CUTS)
        def _(inner):
            slot = index * ROUND + inner % ROUND
            pl.when(slot > 0)(lambda: act(slot, inner // ROUND))

    @pl.loop(0, batches)
    def _(index):
        each_copy(index, lambda slot, part: outward(slot, part).wait_recv())

        @pl.loop(0, ROUND)
        def _(inner):
            values = arrived[slot_rows(index * ROUND + inner), :].astype(jnp.float32)
            size = lax.rsqrt(jnp.mean(values * values, axis=-1, keepdims=True) + EPSILON)
            normed[slot_rows(inner), :] = (values * size * gain[...]).astype(jnp.bfloat16)

        @pl.loop(0, w_gate.shape[1] // 256)
        def _(tile):
            tiles = pl.ds(pl.multiple_of(tile * 256, 256), 256)
            gate = jnp.dot(normed[...], gate_mat[:, tiles], preferred_element_type=jnp.float32)
            up = jnp.dot(normed[...], up_mat[:, tiles], preferred_element_type=jnp.float32)
            hidden[batch_rows(index), tiles] = (gate / (1.0 + jnp.exp(-gate)) * up).astype(
                jnp.bfloat16
            )

        each_copy(index, lambda slot, part: outward(slot, part).wait_send())
        reply(index, 0)

    @pl.loop(batches, CUTS * batches)
    def _(turn):
        reply(turn % batches, turn // batches)

    for index in range(2):
        for step in steps:
            tap_copy(index, step).wait_recv()
    merge_total[...] = jnp.zeros_like(merge_total)

    def add_merge(source, index, part):
        depth = pl.ds(pl.multiple_of(index * D + part * cut, cut), cut)
        merge_total[...] += jnp.dot(
            source[:, columns(part)], merge_mat[depth, :], preferred_element_type=jnp.float32
        )

    @pl.loop(0, CUTS)
    def _(part):
        add_merge(low_rows, 0, part)
        add_merge(mid_rows, 1, part)

    def add_high(part):
        for step in steps:
            high_copy(part, step).wait_recv()
        add_merge(high, 2, part)

    @pl.loop(0, CUTS)
    def _(part):
        total[...] = jnp.zeros_like(total)

        @pl.loop(0, batches)
        def _(index):
            @pl.loop(index * ROUND, (index + 1) * ROUND)
            def _(slot):
                pl.when(slot > 0)(lambda: homeward(slot, part).wait_recv())

            span = batch_rows(index)
            total[...] += jnp.dot(
                shares[:, span], returned[span, columns(part)], preferred_element_type=jnp.float32
            )

        partial[:, columns(part)] = total[...].astype(jnp.bfloat16)
        for step in steps:
            sum_copy(part, step).start()
        mixed = all_tokens[mine, columns(part)].astype(jnp.float32) + total[mine, :]
        for step in steps:
            sum_copy(part, step).wait_recv()
            mixed += halves[step - 1, :, columns(part)].astype(jnp.float32)
        high[mine, columns(part)] = mixed.astype(jnp.bfloat16)
        for step in steps:
            high_copy(part, step).start()
        pl.when(part > 0)(lambda: add_high(part - 1))

    add_high(CUTS - 1)
    merged[...] = merge_total[...].astype(jnp.bfloat16)

    @pl.loop(0, batches)
    def _(index):
        each_copy(index, lambda slot, part: homeward(slot, part).wait_send())

    for step in steps:
        route_copy(step).wait_send()
        tap_copy(2, step).wait_recv()
        for index in range(3):
            tap_copy(index, step).wait_send()

        @pl.loop(0, CUTS)
        def _(part):
            token_copy(part, step).wait_send()
            sum_copy(part, step).wait_send()
            high_copy(part, step).wait_send()


def experts(
    tokens, choices, gates, low, mid, embed, w_gate, w_up, w_down, w_merge, gain, segments, freqs
):
    rows, width, out_width = tokens.shape[0], w_gate.shape[1], w_merge.shape[1]
    everyone = N_X * rows
    slots = CAPACITY * N_X
    hbm = pl.BlockSpec(memory_space=pl.ANY)
    vmem = pl.BlockSpec(memory_space=pltpu.VMEM)
    dma = pltpu.SemaphoreType.DMA

    def half(*shape):
        return pltpu.VMEM(shape, jnp.bfloat16)

    def full(*shape):
        return pltpu.VMEM(shape, jnp.float32)

    few, many = (N_X - 1) * CUTS, PEERS * CUTS
    return pl.pallas_call(
        experts_kernel,
        out_shape=(
            jax.ShapeDtypeStruct((everyone, out_width), jnp.bfloat16),
            jax.ShapeDtypeStruct((everyone, D), jnp.bfloat16),
            jax.ShapeDtypeStruct((everyone, HD), jnp.float32),
            jax.ShapeDtypeStruct((everyone, HD), jnp.float32),
            jax.ShapeDtypeStruct((everyone, 1), jnp.int32),
        ),
        in_specs=[hbm, vmem, vmem] + [hbm] * 7 + [vmem] * 3,
        out_specs=(vmem, hbm, vmem, vmem, vmem),
        scratch_shapes=[
            full(N_X, 2, PEERS, rows),
            full(N_X, 2, PEERS, rows),
            half(PEERS * slots, everyone),
            full(ROUND * slots, everyone),
            half(everyone, PEERS * slots),
            half(everyone, D),
            half(PEERS * slots, D),
            half(PEERS * slots, D),
            half(ROUND * slots, D),
            half(PEERS * slots, width),
            half(PEERS * slots, D),
            full(everyone, D // CUTS),
            half(everyone, D),
            half(N_X - 1, rows, D),
            half(everyone, D),
            half(everyone, D),
            half(everyone, D),
            full(everyone, out_width),
            half(D, width),
            half(D, width),
            half(width, D),
            half(3 * D, out_width),
            dma((9,)),
            dma((N_X - 1,)), dma((N_X - 1,)),
            dma((few,)), dma((few,)),
            dma((many,)), dma((many,)),
            dma((many,)), dma((many,)),
            dma((9,)), dma((9,)),
            dma((few,)), dma((few,)),
            dma((few,)), dma((few,)),
        ],
        compiler_params=pltpu.CompilerParams(
            collective_id=2, has_side_effects=True, vmem_limit_bytes=60 << 20
        ),
        cost_estimate=pl.CostEstimate(
            flops=6 * PEERS * slots * D * width, bytes_accessed=40 << 20, transcendentals=0
        ),
        name="experts",
    )(
        tokens, choices, gates, low, mid, embed, w_gate, w_up, w_down, w_merge, gain, segments, freqs
    )


def draft_kernel(
    merged, embed, w_query, w_kv, embed_gain, merged_gain, q_gain, k_gain, cosine, sine, row_start,
    out,
    pieces, embeds, joined, embed_total, merged_total, squares, query, held, total,
    query_mat, kv_mat,
    x_sends, x_arrivals, z_sends, z_arrivals, y_sends, y_arrivals, core_sends, core_arrivals, own,
):
    rows, cut = merged.shape
    heads = query.shape[0]
    here, x = lax.axis_index("expert"), lax.axis_index("group")
    z, y, core = here // (N_Y * N_CORE), here // N_CORE % N_Y, here % N_CORE
    loads = [
        pltpu.make_async_copy(source, target, own.at[index])
        for index, (source, target) in enumerate(
            ((merged, pieces.at[x]), (embed, embeds), (w_query, query_mat), (w_kv, kv_mat))
        )
    ]
    for load in loads:
        load.start()
    greet(
        [across(step) for step in (1, 2, 3)]
        + [(peer((step, 0, 0)), x) for step in (1, 2, 3)]
        + [(peer((0, step, 0)), x) for step in (1, 2, 3)]
        + [(peer((0, 0, 1)), x)]
    )
    near, far = 1, N_X - 1
    size = rows // len(HALVES)

    def span_of(half):
        return pl.ds(half * size, size)

    def direct(index, half):
        span = span_of(half)
        return remote(
            merged.at[span], pieces.at[x, span], x_sends, x_arrivals, 4 * half + index,
            across((near, far)[index]),
        )

    def onward(index, half):
        block = (x + (far, near)[index]) % N_X
        span = pl.ds(half * size + index * size // 2, size // 2)
        return remote(
            pieces.at[block, span], pieces.at[block, span], x_sends, x_arrivals,
            4 * half + 2 + index, across((near, far)[index]),
        )

    for index in (0, 1):
        direct(index, 0).start()

    def add_part(source, depth, target):
        target[:, : heads * HD] += jnp.dot(
            source, query_mat[depth, :], preferred_element_type=jnp.float32
        )
        target[:, heads * HD :] += jnp.dot(
            source, kv_mat[depth, :], preferred_element_type=jnp.float32
        )

    def columns(part):
        return pl.ds(pl.multiple_of(part * cut, cut), cut)

    embed_total[...] = jnp.zeros_like(embed_total)
    merged_total[...] = jnp.zeros_like(merged_total)
    squares[...] = jnp.zeros_like(squares)
    loads[1].wait()
    chunk = rows // 8

    @pl.loop(0, 8)
    def _(index):
        span = pl.ds(pl.multiple_of(index * chunk, chunk), chunk)
        values = embeds[span, :].astype(jnp.float32)
        size = lax.rsqrt(jnp.mean(values * values, axis=-1, keepdims=True) + EPSILON)
        joined[span, :] = (values * size * embed_gain[...]).astype(jnp.bfloat16)

    for index in (0, 1):
        direct(index, 0).wait_recv()
        onward(index, 0).start()
        direct(index, 1).start()
    for load in (loads[0], loads[2], loads[3]):
        load.wait()

    @pl.loop(0, N_X)
    def _(part):
        add_part(joined[:, columns(part)], columns(part), embed_total)

    def add_piece(block, half):
        span = span_of(half)
        values = pieces[block, span].astype(jnp.float32)
        squares[span, :] += jnp.broadcast_to(
            jnp.sum(values * values, axis=-1, keepdims=True), (size, HD)
        )
        source = (values * merged_gain[:, columns(block)]).astype(jnp.bfloat16)
        joined[span, columns(block)] = source
        depth = pl.ds(pl.multiple_of(D + block * cut, cut), cut)
        merged_total[span, heads * HD :] += jnp.dot(
            source, kv_mat[depth, :], preferred_element_type=jnp.float32
        )

    def project(index, span):
        shrink = lax.rsqrt(squares[span, :1] * (1.0 / D) + EPSILON)
        lanes = slice(index * HD, (index + 1) * HD)
        return embed_total[span, lanes] + merged_total[span, lanes] * shrink

    def turned(values, gain, span):
        scale = lax.rsqrt(jnp.mean(values * values, axis=-1, keepdims=True) + EPSILON)
        values = values * scale * gain[...]
        return values * cosine[span, :] + pltpu.roll(values, HD // 2, 1) * sine[span, :]

    def place(plane, row, column):
        return (plane * N_Y + row) * N_CORE + column

    def wanted(plane, row, reader):
        near = (plane == 0) & (row <= reader)
        return near | ((plane == 1) & (z >= 1)) | ((plane == 2) & (z >= 2) & (row >= reader))

    def along_z(plane, half):
        span = span_of(half)
        return remote(
            held.at[place(0, y, core), :, span], held.at[place(plane, y, core), :, span],
            z_sends, z_arrivals, 2 * (plane - 1) + half, (peer((plane, 0, 0)), x),
        )

    def along_y(plane, step, half):
        part = held.at[place(plane, y, core), :, span_of(half)]
        return remote(
            part, part, y_sends, y_arrivals, 2 * (3 * plane + step - 1) + half,
            (peer((0, step, 0)), x),
        )

    def from_y(plane, step, row, half):
        part = held.at[place(plane, row, core), :, span_of(half)]
        return remote(
            part, part, y_sends, y_arrivals, 2 * (3 * plane + step - 1) + half,
            (peer((0, 1, 0)), x),
        )

    def sibling(plane, row, column, half):
        part = held.at[place(plane, row, column), :, span_of(half)]
        return remote(
            part, part, core_sends, core_arrivals, 2 * (N_Y * plane + row) + half,
            (peer((0, 0, 1)), x),
        )

    def share(plane, half):
        for step in (1, 2, 3):
            pl.when(wanted(plane, y, (y + step) % N_Y))(along_y(plane, step, half).start)

    total[...] = jnp.zeros_like(total)
    for half in HALVES:
        for turn in (0, 3, 1):
            add_piece((x + turn) % N_X, half)
        if half == 0:
            for index in (0, 1):
                direct(index, 1).wait_recv()
                onward(index, 1).start()
        for index in (0, 1):
            onward(index, half).wait_recv()
        add_piece((x + 2) % N_X, half)
        span = span_of(half)
        mine = place(0, y, core)
        held[mine, 0, span] = turned(project(heads, span), k_gain, span).astype(jnp.bfloat16)
        held[mine, 1, span] = project(heads + 1, span).astype(jnp.bfloat16)
        for plane in (2, 1):
            pl.when(z + plane < N_Z)(along_z(plane, half).start)
        share(0, half)
        sibling(0, y, core, half).start()

    def pass_plane(plane, half):
        @pl.when(z >= plane)
        def _():
            along_z(plane, half).wait_recv()
            share(plane, half)
            pl.when(wanted(plane, y, y))(sibling(plane, y, core, half).start)

    pass_plane(1, 0)

    @pl.loop(0, N_X)
    def _(part):
        depth = pl.ds(pl.multiple_of(D + part * cut, cut), cut)
        merged_total[:, : heads * HD] += jnp.dot(
            joined[:, columns(part)], query_mat[depth, :], preferred_element_type=jnp.float32
        )

    everything = pl.ds(0, rows)
    for index in range(heads):
        query[index] = (
            turned(project(index, everything), q_gain, everything) * (HD**-0.5 * LOG2E)
        ).astype(jnp.bfloat16)

    def add_block(plane, row, column):
        slot = place(plane, row, column)
        first = ((z - plane) * N_Y * N_CORE + row * N_CORE + column) * rows
        key = held[slot, 0]
        value = jnp.concatenate([held[slot, 1], jnp.ones((rows, HD), jnp.bfloat16)], axis=1)
        query_index = here * rows + lax.broadcasted_iota(jnp.int32, (rows, rows), 0)
        key_index = first + lax.broadcasted_iota(jnp.int32, (rows, rows), 1)
        allowed = (key_index <= query_index) & (key_index >= row_start[...])
        for head in range(heads):
            scores = lax.dot_general(
                query[head], key, (((1,), (1,)), ((), ())), preferred_element_type=jnp.float32
            )
            weights = jnp.where(allowed, jnp.exp2(scores), 0.0).astype(jnp.bfloat16)
            total[head] += jnp.dot(weights, value, preferred_element_type=jnp.float32)

    def needed(plane, row, column):
        behind = here - ((z - plane) * N_Y * N_CORE + row * N_CORE + column)
        return wanted(plane, row, y) & (behind >= 0) & (behind <= WINDOW)

    pass_plane(1, 1)
    add_block(0, y, core)
    for half in HALVES:
        pass_plane(2, half)

    @pl.loop(1, 3 * N_Y + 1)
    def _(step):
        plane, back = step // N_Y, step % N_Y
        row = (y + N_Y - back) % N_Y

        @pl.when((step < 3 * N_Y) & wanted(plane, row, y))
        def _():
            @pl.when(back > 0)
            def _():
                for half in HALVES:
                    from_y(plane, back, row, half).wait_recv()
                    sibling(plane, row, core, half).start()

            pl.when(needed(plane, row, core))(lambda: add_block(plane, row, core))

        plane, back = (step - 1) // N_Y, (step - 1) % N_Y
        row = (y + N_Y - back) % N_Y

        @pl.when(wanted(plane, row, y))
        def _():
            for half in HALVES:
                sibling(plane, row, 1 - core, half).wait_recv()
            pl.when(needed(plane, row, 1 - core))(lambda: add_block(plane, row, 1 - core))

    for head in range(heads):
        out[:, head * HD : (head + 1) * HD] = (
            total[head, :, :HD] / total[head, :, HD:]
        ).astype(out.dtype)
    for half in HALVES:
        for plane in (1, 2):
            pl.when(z + plane < N_Z)(along_z(plane, half).wait_send)
        for plane in (0, 1, 2):
            for step in (1, 2, 3):
                pl.when(wanted(plane, y, (y + step) % N_Y))(along_y(plane, step, half).wait_send)
            for row in range(N_Y):
                pl.when(wanted(plane, row, y))(sibling(plane, row, core, half).wait_send)
        for index in (0, 1):
            direct(index, half).wait_send()
            onward(index, half).wait_send()


def draft(merged, embed, w_query, w_kv, embed_gain, merged_gain, q_gain, k_gain, cosine, sine, row_start):
    rows, cut = merged.shape
    heads = w_query.shape[1] // HD
    wide = w_query.shape[1] + w_kv.shape[1]
    hbm = pl.BlockSpec(memory_space=pl.ANY)
    vmem = pl.BlockSpec(memory_space=pltpu.VMEM)
    dma = pltpu.SemaphoreType.DMA
    return pl.pallas_call(
        draft_kernel,
        out_shape=jax.ShapeDtypeStruct((rows, heads * HD), jnp.bfloat16),
        in_specs=[hbm] * 4 + [vmem] * 7,
        out_specs=vmem,
        scratch_shapes=[
            pltpu.VMEM((N_X, rows, cut), jnp.bfloat16),
            pltpu.VMEM((rows, D), jnp.bfloat16),
            pltpu.VMEM((rows, D), jnp.bfloat16),
            pltpu.VMEM((rows, wide), jnp.float32),
            pltpu.VMEM((rows, wide), jnp.float32),
            pltpu.VMEM((rows, HD), jnp.float32),
            pltpu.VMEM((heads, rows, HD), jnp.bfloat16),
            pltpu.VMEM((3 * N_Y * N_CORE, 2, rows, HD), jnp.bfloat16),
            pltpu.VMEM((heads, rows, 2 * HD), jnp.float32),
            pltpu.VMEM((2 * D, heads * HD), jnp.bfloat16),
            pltpu.VMEM((2 * D, w_kv.shape[1]), jnp.bfloat16),
            dma((8,)), dma((8,)), dma((4,)), dma((4,)), dma((18,)), dma((18,)), dma((24,)), dma((24,)),
            dma((4,)),
        ],
        compiler_params=pltpu.CompilerParams(
            collective_id=3, has_side_effects=True, vmem_limit_bytes=56 << 20
        ),
        name="draft",
    )(
        merged, embed, w_query, w_kv, embed_gain[None, :], merged_gain[None, :], q_gain[None, :],
        k_gain[None, :], cosine, sine, row_start,
    )


def body(
    tokens,
    low_tap,
    mid_tap,
    next_embed,
    expert_ids,
    gate_weights,
    segments,
    moe_gain,
    w_gate,
    w_up,
    w_down,
    merge_weight,
    embed_gain,
    merged_gain,
    w_query,
    w_kv,
    q_gain,
    k_gain,
):
    half = HD // 2
    freqs = np.power(THETA, -np.arange(half) * 2.0 / HD).astype(np.float32)
    freqs = np.concatenate([freqs, freqs])[None, :]
    merged, embed_rows, cosine, sine, row_start = experts(
        tokens, expert_ids.T, gate_weights.T, low_tap, mid_tap, next_embed, w_gate[0], w_up[0],
        w_down[0], merge_weight, moe_gain[None, :], segments.reshape(-1, HD), jnp.asarray(freqs),
    )
    return draft(
        merged, embed_rows, w_query, w_kv.reshape(w_kv.shape[0], -1), embed_gain, merged_gain,
        q_gain, k_gain, cosine, sine, row_start,
    )


def solution(mesh):
    return jax.shard_map(
        body,
        mesh=mesh,
        in_specs=(
            P(("expert", "group"), None),
            P(("expert", "group"), None),
            P(("expert", "group"), None),
            P(("expert", "group"), None),
            P(("expert", "group"), None),
            P(("expert", "group"), None),
            P(),
            P(),
            P(("expert", "group"), None, None),
            P(("expert", "group"), None, None),
            P(("expert", "group"), None, None),
            P(None, "group"),
            P(),
            P(),
            P(None, "group"),
            P(None, None, "group"),
            P(),
            P(),
        ),
        out_specs=P("expert", "group"),
        check_vma=False,
    )
```

```python
import jax
import jax.numpy as jnp
import numpy as np
from jax import lax
from jax.experimental import pallas as pl
from jax.experimental.pallas import tpu as pltpu
from jax.sharding import PartitionSpec as P

D = 2048
HD = 128
TOPK = 8
SEGS = 4


EPSILON = 1e-06
THETA = 1000000.0
LOG2E = 1.4426950408889634
MESH = pl.DeviceIdType.MESH
N_Z, N_Y, N_CORE, N_X = 4, 4, 2, 4
PEERS = N_Z * N_Y * N_CORE
ROUND = 8
WINDOW = 16
CUTS = 4
HALVES = (0, 1)
CAPACITY = 12
NOWHERE = -1000.0


def offset_of(slot):
    turn = slot // N_CORE
    return ((turn // N_Y + turn) % N_Z, turn % N_Y, slot % N_CORE)


def peer(offset, sign=1):
    here = lax.axis_index("expert")
    z = (here // (N_Y * N_CORE) + sign * offset[0] + N_Z) % N_Z
    y = (here // N_CORE % N_Y + sign * offset[1] + N_Y) % N_Y
    core = (here + offset[2]) % N_CORE
    return (z * N_Y + y) * N_CORE + core


def remote(source, target, sends, arrivals, slot, device):
    return pltpu.make_async_remote_copy(
        src_ref=source,
        dst_ref=target,
        send_sem=sends.at[slot],
        recv_sem=arrivals.at[slot],
        device_id=device,
        device_id_type=MESH,
    )


def greet(devices):
    barrier = pltpu.get_barrier_semaphore()
    for device in devices:
        pl.semaphore_signal(barrier, inc=1, device_id=device, device_id_type=MESH)
    pl.semaphore_wait(barrier, len(devices))


def across(step):
    return (lax.axis_index("expert"), (lax.axis_index("group") + step) % N_X)


def experts_kernel(
    tokens, choices, gates, low, mid, embed, w_gate, w_up, w_down, w_merge, gain, segments, freqs,
    merged, embed_rows, cosine, sine, row_start,
    routing, route, place, weights, shares, all_tokens, packed, arrived, normed, hidden, returned,
    total, partial, halves, high, low_rows, mid_rows, merge_total,
    gate_mat, up_mat, down_mat, merge_mat,
    own, route_sends, route_arrivals, token_sends, token_arrivals, out_sends, out_arrivals,
    back_sends, back_arrivals, tap_sends, tap_arrivals, sum_sends, sum_arrivals,
    high_sends, high_arrivals,
):
    x = lax.axis_index("group")
    rows = tokens.shape[0]
    slots = CAPACITY * N_X
    batch = ROUND * slots
    batches = PEERS // ROUND
    cut = D // CUTS
    steps = range(1, N_X)
    mine = pl.ds(pl.multiple_of(x * rows, rows), rows)

    def columns(part):
        return pl.ds(pl.multiple_of(part * cut, cut), cut)

    def slot_rows(slot):
        return pl.ds(pl.multiple_of(slot * slots, slots), slots)

    def batch_rows(index):
        return pl.ds(pl.multiple_of(index * batch, batch), batch)

    kept = [
        pltpu.make_async_copy(source, target, own.at[index])
        for index, (source, target) in enumerate(
            (
                (tokens, all_tokens.at[mine]),
                (w_gate, gate_mat),
                (w_up, up_mat),
                (w_down, down_mat),
                (low, low_rows.at[mine]),
                (mid, mid_rows.at[mine]),
                (w_merge, merge_mat),
                (embed, embed_rows.at[mine]),
            )
        )
    ]
    for copy in kept:
        copy.start()

    barrier = pltpu.get_barrier_semaphore()
    for step in steps:
        pl.semaphore_signal(barrier, inc=1, device_id=across(step), device_id_type=MESH)

    @pl.loop(1, PEERS)
    def _(slot):
        pl.semaphore_signal(
            barrier, inc=1, device_id=(peer(offset_of(slot), -1), x), device_id_type=MESH
        )

    slot = lax.broadcasted_iota(jnp.int32, (PEERS, 1), 0)
    owner = peer(offset_of(slot)) * N_X
    earlier = lax.broadcasted_iota(jnp.int32, (rows, rows), 0) < lax.broadcasted_iota(
        jnp.int32, (rows, rows), 1
    )
    earlier = jnp.where(earlier, 1.0, 0.0).astype(jnp.bfloat16)
    for plane in range(N_X):
        member = jnp.zeros((PEERS, rows), jnp.float32)
        share = jnp.zeros((PEERS, rows), jnp.float32)
        for choice in range(TOPK):
            hit = choices[choice : choice + 1, :] == owner + plane
            member += jnp.where(hit, 1.0, 0.0)
            share += jnp.where(hit, gates[choice : choice + 1, :], 0.0)
        ranks = jnp.dot(member.astype(jnp.bfloat16), earlier, preferred_element_type=jnp.float32)
        shift = (CAPACITY * x).astype(jnp.float32)
        routing[plane, 0] = jnp.where(member > 0.0, ranks + shift, NOWHERE)
        routing[plane, 1] = share

    pl.semaphore_wait(barrier, PEERS - 1 + N_X - 1)

    def route_copy(step):
        return remote(
            routing.at[(x + step) % N_X], route.at[x], route_sends, route_arrivals, step - 1,
            across(step),
        )

    def token_copy(part, step):
        return remote(
            tokens.at[:, columns(part)], all_tokens.at[mine, columns(part)],
            token_sends, token_arrivals, (N_X - 1) * part + step - 1, across(step),
        )

    def outward(slot, part):
        return remote(
            packed.at[slot_rows(slot), columns(part)], arrived.at[slot_rows(slot), columns(part)],
            out_sends, out_arrivals, PEERS * part + slot, (peer(offset_of(slot)), x),
        )

    def homeward(slot, part):
        return remote(
            packed.at[slot_rows(slot), columns(part)], returned.at[slot_rows(slot), columns(part)],
            back_sends, back_arrivals, PEERS * part + slot, (peer(offset_of(slot), -1), x),
        )

    def tap_copy(index, step):
        source = (low, mid, embed)[index]
        target = (low_rows, mid_rows, embed_rows)[index]
        return remote(
            source, target.at[mine], tap_sends, tap_arrivals, (N_X - 1) * index + step - 1,
            across(step),
        )

    def sum_copy(part, step):
        theirs = pl.ds(pl.multiple_of((x + step) % N_X * rows, rows), rows)
        return remote(
            partial.at[theirs, columns(part)], halves.at[step - 1, :, columns(part)],
            sum_sends, sum_arrivals, (N_X - 1) * part + step - 1, across(step),
        )

    def high_copy(part, step):
        return remote(
            high.at[mine, columns(part)], high.at[mine, columns(part)],
            high_sends, high_arrivals, (N_X - 1) * part + step - 1, across(step),
        )

    for step in steps:
        route_copy(step).start()
    for part in range(2):
        for step in steps:
            token_copy(part, step).start()
    route[x] = routing[x]
    for step in steps:
        route_copy(step).wait_recv()

    def spread_line(kind, slot):
        return jnp.concatenate(
            [route[block, kind, pl.ds(slot, 1), :] for block in range(N_X)], axis=1
        )

    def match(slot):
        lines = lax.broadcasted_iota(jnp.int32, (slots, N_X * rows), 0).astype(jnp.float32)
        return lines == spread_line(0, slot)

    @pl.loop(0, PEERS)
    def _(slot):
        place[slot_rows(slot), :] = jnp.where(match(slot), 1.0, 0.0).astype(jnp.bfloat16)

    kept[0].wait()

    @pl.loop(0, CUTS)
    def _(part):
        for step in steps:
            token_copy(part, step).wait_recv()

        @pl.when(part + 2 < CUTS)
        def _():
            for step in steps:
                token_copy(part + 2, step).start()

        @pl.loop(0, batches)
        def _(index):
            span = batch_rows(index)
            packed[span, columns(part)] = jnp.dot(
                place[span, :], all_tokens[:, columns(part)], preferred_element_type=jnp.float32
            ).astype(jnp.bfloat16)

            @pl.loop(index * ROUND, (index + 1) * ROUND)
            def _(slot):
                pl.when(slot > 0)(lambda: outward(slot, part).start())

        arrived[slot_rows(0), columns(part)] = packed[slot_rows(0), columns(part)]

    for index in range(3):
        for step in steps:
            tap_copy(index, step).start()

    @pl.loop(0, batches)
    def _(index):
        @pl.loop(0, ROUND)
        def _(inner):
            slot = index * ROUND + inner
            weights[slot_rows(inner), :] = jnp.where(match(slot), spread_line(1, slot), 0.0)

        shares[:, batch_rows(index)] = weights[...].T.astype(jnp.bfloat16)

    line = lax.axis_index("expert") * N_X * rows + lax.broadcasted_iota(
        jnp.int32, (N_X * rows, 1), 0
    )
    line = line.astype(jnp.float32)
    start = jnp.zeros_like(line)
    for label in range(1, SEGS):
        below = jnp.where(segments[...] < label, 1.0, 0.0)
        count = jnp.sum(jnp.sum(below, axis=1, keepdims=True), axis=0, keepdims=True)
        start = jnp.maximum(start, jnp.where(count <= line, count, 0.0))
    row_start[...] = start.astype(jnp.int32)
    angles = (line - start) * freqs[...]
    signs = jnp.where(lax.broadcasted_iota(jnp.int32, (1, HD), 1) < HD // 2, -1.0, 1.0)
    cosine[...] = jnp.cos(angles)
    sine[...] = jnp.sin(angles) * signs
    for copy in kept[1:]:
        copy.wait()

    def reply(index, part):
        span = batch_rows(index)
        packed[span, columns(part)] = jnp.dot(
            hidden[span, :], down_mat[:, columns(part)], preferred_element_type=jnp.float32
        ).astype(jnp.bfloat16)

        @pl.loop(index * ROUND, (index + 1) * ROUND)
        def _(slot):
            pl.when(slot > 0)(lambda: homeward(slot, part).start())

        @pl.when(index == 0)
        def _():
            returned[slot_rows(0), columns(part)] = packed[slot_rows(0), columns(part)]

    def each_copy(index, act):
        @pl.loop(0, ROUND * CUTS)
        def _(inner):
            slot = index * ROUND + inner % ROUND
            pl.when(slot > 0)(lambda: act(slot, inner // ROUND))

    @pl.loop(0, batches)
    def _(index):
        each_copy(index, lambda slot, part: outward(slot, part).wait_recv())

        @pl.loop(0, ROUND)
        def _(inner):
            values = arrived[slot_rows(index * ROUND + inner), :].astype(jnp.float32)
            size = lax.rsqrt(jnp.mean(values * values, axis=-1, keepdims=True) + EPSILON)
            normed[slot_rows(inner), :] = (values * size * gain[...]).astype(jnp.bfloat16)

        @pl.loop(0, w_gate.shape[1] // 256)
        def _(tile):
            tiles = pl.ds(pl.multiple_of(tile * 256, 256), 256)
            gate = jnp.dot(normed[...], gate_mat[:, tiles], preferred_element_type=jnp.float32)
            up = jnp.dot(normed[...], up_mat[:, tiles], preferred_element_type=jnp.float32)
            hidden[batch_rows(index), tiles] = (gate / (1.0 + jnp.exp(-gate)) * up).astype(
                jnp.bfloat16
            )

        each_copy(index, lambda slot, part: outward(slot, part).wait_send())
        reply(index, 0)

    @pl.loop(batches, CUTS * batches)
    def _(turn):
        reply(turn % batches, turn // batches)

    for index in range(2):
        for step in steps:
            tap_copy(index, step).wait_recv()
    merge_total[...] = jnp.zeros_like(merge_total)

    def add_merge(source, index, part):
        depth = pl.ds(pl.multiple_of(index * D + part * cut, cut), cut)
        merge_total[...] += jnp.dot(
            source[:, columns(part)], merge_mat[depth, :], preferred_element_type=jnp.float32
        )

    @pl.loop(0, CUTS)
    def _(part):
        add_merge(low_rows, 0, part)
        add_merge(mid_rows, 1, part)

    def add_high(part):
        for step in steps:
            high_copy(part, step).wait_recv()
        add_merge(high, 2, part)

    @pl.loop(0, CUTS)
    def _(part):
        total[...] = jnp.zeros_like(total)

        @pl.loop(0, batches)
        def _(index):
            @pl.loop(index * ROUND, (index + 1) * ROUND)
            def _(slot):
                pl.when(slot > 0)(lambda: homeward(slot, part).wait_recv())

            span = batch_rows(index)
            total[...] += jnp.dot(
                shares[:, span], returned[span, columns(part)], preferred_element_type=jnp.float32
            )

        partial[:, columns(part)] = total[...].astype(jnp.bfloat16)
        for step in steps:
            sum_copy(part, step).start()
        mixed = all_tokens[mine, columns(part)].astype(jnp.float32) + total[mine, :]
        for step in steps:
            sum_copy(part, step).wait_recv()
            mixed += halves[step - 1, :, columns(part)].astype(jnp.float32)
        high[mine, columns(part)] = mixed.astype(jnp.bfloat16)
        for step in steps:
            high_copy(part, step).start()
        pl.when(part > 0)(lambda: add_high(part - 1))

    add_high(CUTS - 1)
    merged[...] = merge_total[...].astype(jnp.bfloat16)

    @pl.loop(0, batches)
    def _(index):
        each_copy(index, lambda slot, part: homeward(slot, part).wait_send())

    for step in steps:
        route_copy(step).wait_send()
        tap_copy(2, step).wait_recv()
        for index in range(3):
            tap_copy(index, step).wait_send()

        @pl.loop(0, CUTS)
        def _(part):
            token_copy(part, step).wait_send()
            sum_copy(part, step).wait_send()
            high_copy(part, step).wait_send()


def experts(
    tokens, choices, gates, low, mid, embed, w_gate, w_up, w_down, w_merge, gain, segments, freqs
):
    rows, width, out_width = tokens.shape[0], w_gate.shape[1], w_merge.shape[1]
    everyone = N_X * rows
    slots = CAPACITY * N_X
    hbm = pl.BlockSpec(memory_space=pl.ANY)
    vmem = pl.BlockSpec(memory_space=pltpu.VMEM)
    dma = pltpu.SemaphoreType.DMA

    def half(*shape):
        return pltpu.VMEM(shape, jnp.bfloat16)

    def full(*shape):
        return pltpu.VMEM(shape, jnp.float32)

    few, many = (N_X - 1) * CUTS, PEERS * CUTS
    return pl.pallas_call(
        experts_kernel,
        out_shape=(
            jax.ShapeDtypeStruct((everyone, out_width), jnp.bfloat16),
            jax.ShapeDtypeStruct((everyone, D), jnp.bfloat16),
            jax.ShapeDtypeStruct((everyone, HD), jnp.float32),
            jax.ShapeDtypeStruct((everyone, HD), jnp.float32),
            jax.ShapeDtypeStruct((everyone, 1), jnp.int32),
        ),
        in_specs=[hbm, vmem, vmem] + [hbm] * 7 + [vmem] * 3,
        out_specs=(vmem, hbm, vmem, vmem, vmem),
        scratch_shapes=[
            full(N_X, 2, PEERS, rows),
            full(N_X, 2, PEERS, rows),
            half(PEERS * slots, everyone),
            full(ROUND * slots, everyone),
            half(everyone, PEERS * slots),
            half(everyone, D),
            half(PEERS * slots, D),
            half(PEERS * slots, D),
            half(ROUND * slots, D),
            half(PEERS * slots, width),
            half(PEERS * slots, D),
            full(everyone, D // CUTS),
            half(everyone, D),
            half(N_X - 1, rows, D),
            half(everyone, D),
            half(everyone, D),
            half(everyone, D),
            full(everyone, out_width),
            half(D, width),
            half(D, width),
            half(width, D),
            half(3 * D, out_width),
            dma((9,)),
            dma((N_X - 1,)), dma((N_X - 1,)),
            dma((few,)), dma((few,)),
            dma((many,)), dma((many,)),
            dma((many,)), dma((many,)),
            dma((9,)), dma((9,)),
            dma((few,)), dma((few,)),
            dma((few,)), dma((few,)),
        ],
        compiler_params=pltpu.CompilerParams(
            collective_id=2, has_side_effects=True, vmem_limit_bytes=60 << 20
        ),
        cost_estimate=pl.CostEstimate(
            flops=6 * PEERS * slots * D * width, bytes_accessed=40 << 20, transcendentals=0
        ),
        name="experts",
    )(
        tokens, choices, gates, low, mid, embed, w_gate, w_up, w_down, w_merge, gain, segments, freqs
    )


def draft_kernel(
    merged, embed, w_query, w_kv, embed_gain, merged_gain, q_gain, k_gain, cosine, sine, row_start,
    out,
    pieces, embeds, joined, embed_total, merged_total, squares, query, held, total,
    query_mat, kv_mat,
    x_sends, x_arrivals, z_sends, z_arrivals, y_sends, y_arrivals, core_sends, core_arrivals, own,
):
    rows, cut = merged.shape
    heads = query.shape[0]
    here, x = lax.axis_index("expert"), lax.axis_index("group")
    z, y, core = here // (N_Y * N_CORE), here // N_CORE % N_Y, here % N_CORE
    loads = [
        pltpu.make_async_copy(source, target, own.at[index])
        for index, (source, target) in enumerate(
            ((merged, pieces.at[x]), (embed, embeds), (w_query, query_mat), (w_kv, kv_mat))
        )
    ]
    for load in loads:
        load.start()
    greet(
        [across(step) for step in (1, 2, 3)]
        + [(peer((step, 0, 0)), x) for step in (1, 2, 3)]
        + [(peer((0, step, 0)), x) for step in (1, 2, 3)]
        + [(peer((0, 0, 1)), x)]
    )
    near, far = 1, N_X - 1
    size = rows // len(HALVES)

    def span_of(half):
        return pl.ds(half * size, size)

    def direct(index, half):
        span = span_of(half)
        return remote(
            merged.at[span], pieces.at[x, span], x_sends, x_arrivals, 4 * half + index,
            across((near, far)[index]),
        )

    def onward(index, half):
        block = (x + (far, near)[index]) % N_X
        span = pl.ds(half * size + index * size // 2, size // 2)
        return remote(
            pieces.at[block, span], pieces.at[block, span], x_sends, x_arrivals,
            4 * half + 2 + index, across((near, far)[index]),
        )

    for index in (0, 1):
        direct(index, 0).start()

    def add_part(source, depth, target):
        target[:, : heads * HD] += jnp.dot(
            source, query_mat[depth, :], preferred_element_type=jnp.float32
        )
        target[:, heads * HD :] += jnp.dot(
            source, kv_mat[depth, :], preferred_element_type=jnp.float32
        )

    def columns(part):
        return pl.ds(pl.multiple_of(part * cut, cut), cut)

    embed_total[...] = jnp.zeros_like(embed_total)
    merged_total[...] = jnp.zeros_like(merged_total)
    squares[...] = jnp.zeros_like(squares)
    loads[1].wait()
    chunk = rows // 8

    @pl.loop(0, 8)
    def _(index):
        span = pl.ds(pl.multiple_of(index * chunk, chunk), chunk)
        values = embeds[span, :].astype(jnp.float32)
        size = lax.rsqrt(jnp.mean(values * values, axis=-1, keepdims=True) + EPSILON)
        joined[span, :] = (values * size * embed_gain[...]).astype(jnp.bfloat16)

    for index in (0, 1):
        direct(index, 0).wait_recv()
        onward(index, 0).start()
        direct(index, 1).start()
    for load in (loads[0], loads[2], loads[3]):
        load.wait()

    @pl.loop(0, N_X)
    def _(part):
        add_part(joined[:, columns(part)], columns(part), embed_total)

    def add_piece(block, half):
        span = span_of(half)
        values = pieces[block, span].astype(jnp.float32)
        squares[span, :] += jnp.broadcast_to(
            jnp.sum(values * values, axis=-1, keepdims=True), (size, HD)
        )
        source = (values * merged_gain[:, columns(block)]).astype(jnp.bfloat16)
        joined[span, columns(block)] = source
        depth = pl.ds(pl.multiple_of(D + block * cut, cut), cut)
        merged_total[span, heads * HD :] += jnp.dot(
            source, kv_mat[depth, :], preferred_element_type=jnp.float32
        )

    def project(index, span):
        shrink = lax.rsqrt(squares[span, :1] * (1.0 / D) + EPSILON)
        lanes = slice(index * HD, (index + 1) * HD)
        return embed_total[span, lanes] + merged_total[span, lanes] * shrink

    def turned(values, gain, span):
        scale = lax.rsqrt(jnp.mean(values * values, axis=-1, keepdims=True) + EPSILON)
        values = values * scale * gain[...]
        return values * cosine[span, :] + pltpu.roll(values, HD // 2, 1) * sine[span, :]

    def place(plane, row, column):
        return (plane * N_Y + row) * N_CORE + column

    def wanted(plane, row, reader):
        near = (plane == 0) & (row <= reader)
        return near | ((plane == 1) & (z >= 1)) | ((plane == 2) & (z >= 2) & (row >= reader))

    def along_z(plane, half):
        span = span_of(half)
        return remote(
            held.at[place(0, y, core), :, span], held.at[place(plane, y, core), :, span],
            z_sends, z_arrivals, 2 * (plane - 1) + half, (peer((plane, 0, 0)), x),
        )

    def along_y(plane, step, half):
        part = held.at[place(plane, y, core), :, span_of(half)]
        return remote(
            part, part, y_sends, y_arrivals, 2 * (3 * plane + step - 1) + half,
            (peer((0, step, 0)), x),
        )

    def from_y(plane, step, row, half):
        part = held.at[place(plane, row, core), :, span_of(half)]
        return remote(
            part, part, y_sends, y_arrivals, 2 * (3 * plane + step - 1) + half,
            (peer((0, 1, 0)), x),
        )

    def sibling(plane, row, column, half):
        part = held.at[place(plane, row, column), :, span_of(half)]
        return remote(
            part, part, core_sends, core_arrivals, 2 * (N_Y * plane + row) + half,
            (peer((0, 0, 1)), x),
        )

    def share(plane, half):
        for step in (1, 2, 3):
            pl.when(wanted(plane, y, (y + step) % N_Y))(along_y(plane, step, half).start)

    total[...] = jnp.zeros_like(total)
    for half in HALVES:
        for turn in (0, 3, 1):
            add_piece((x + turn) % N_X, half)
        if half == 0:
            for index in (0, 1):
                direct(index, 1).wait_recv()
                onward(index, 1).start()
        for index in (0, 1):
            onward(index, half).wait_recv()
        add_piece((x + 2) % N_X, half)
        span = span_of(half)
        mine = place(0, y, core)
        held[mine, 0, span] = turned(project(heads, span), k_gain, span).astype(jnp.bfloat16)
        held[mine, 1, span] = project(heads + 1, span).astype(jnp.bfloat16)
        for plane in (2, 1):
            pl.when(z + plane < N_Z)(along_z(plane, half).start)
        share(0, half)
        sibling(0, y, core, half).start()

    def pass_plane(plane, half):
        @pl.when(z >= plane)
        def _():
            along_z(plane, half).wait_recv()
            share(plane, half)
            pl.when(wanted(plane, y, y))(sibling(plane, y, core, half).start)

    pass_plane(1, 0)

    @pl.loop(0, N_X)
    def _(part):
        depth = pl.ds(pl.multiple_of(D + part * cut, cut), cut)
        merged_total[:, : heads * HD] += jnp.dot(
            joined[:, columns(part)], query_mat[depth, :], preferred_element_type=jnp.float32
        )

    everything = pl.ds(0, rows)
    for index in range(heads):
        query[index] = (
            turned(project(index, everything), q_gain, everything) * (HD**-0.5 * LOG2E)
        ).astype(jnp.bfloat16)

    def add_block(plane, row, column):
        slot = place(plane, row, column)
        first = ((z - plane) * N_Y * N_CORE + row * N_CORE + column) * rows
        key = held[slot, 0]
        value = jnp.concatenate([held[slot, 1], jnp.ones((rows, HD), jnp.bfloat16)], axis=1)
        query_index = here * rows + lax.broadcasted_iota(jnp.int32, (rows, rows), 0)
        key_index = first + lax.broadcasted_iota(jnp.int32, (rows, rows), 1)
        allowed = (key_index <= query_index) & (key_index >= row_start[...])
        for head in range(heads):
            scores = lax.dot_general(
                query[head], key, (((1,), (1,)), ((), ())), preferred_element_type=jnp.float32
            )
            weights = jnp.where(allowed, jnp.exp2(scores), 0.0).astype(jnp.bfloat16)
            total[head] += jnp.dot(weights, value, preferred_element_type=jnp.float32)

    def needed(plane, row, column):
        behind = here - ((z - plane) * N_Y * N_CORE + row * N_CORE + column)
        return wanted(plane, row, y) & (behind >= 0) & (behind <= WINDOW)

    pass_plane(1, 1)
    add_block(0, y, core)
    @pl.loop(1, 3 * N_Y + 1)
    def _(step):
        @pl.when(step == jnp.where(y == 0, 2 * N_Y, N_Y))
        def _():
            for half in HALVES:
                pass_plane(2, half)

        plane, back = step // N_Y, step % N_Y
        row = (y + N_Y - back) % N_Y

        @pl.when((step < 3 * N_Y) & wanted(plane, row, y))
        def _():
            @pl.when(back > 0)
            def _():
                for half in HALVES:
                    from_y(plane, back, row, half).wait_recv()
                    sibling(plane, row, core, half).start()

            pl.when(needed(plane, row, core))(lambda: add_block(plane, row, core))

        plane, back = (step - 1) // N_Y, (step - 1) % N_Y
        row = (y + N_Y - back) % N_Y

        @pl.when(wanted(plane, row, y))
        def _():
            for half in HALVES:
                sibling(plane, row, 1 - core, half).wait_recv()
            pl.when(needed(plane, row, 1 - core))(lambda: add_block(plane, row, 1 - core))

    for head in range(heads):
        out[:, head * HD : (head + 1) * HD] = (
            total[head, :, :HD] / total[head, :, HD:]
        ).astype(out.dtype)
    for half in HALVES:
        for plane in (1, 2):
            pl.when(z + plane < N_Z)(along_z(plane, half).wait_send)
        for plane in (0, 1, 2):
            for step in (1, 2, 3):
                pl.when(wanted(plane, y, (y + step) % N_Y))(along_y(plane, step, half).wait_send)
            for row in range(N_Y):
                pl.when(wanted(plane, row, y))(sibling(plane, row, core, half).wait_send)
        for index in (0, 1):
            direct(index, half).wait_send()
            onward(index, half).wait_send()


def draft(merged, embed, w_query, w_kv, embed_gain, merged_gain, q_gain, k_gain, cosine, sine, row_start):
    rows, cut = merged.shape
    heads = w_query.shape[1] // HD
    wide = w_query.shape[1] + w_kv.shape[1]
    hbm = pl.BlockSpec(memory_space=pl.ANY)
    vmem = pl.BlockSpec(memory_space=pltpu.VMEM)
    dma = pltpu.SemaphoreType.DMA
    return pl.pallas_call(
        draft_kernel,
        out_shape=jax.ShapeDtypeStruct((rows, heads * HD), jnp.bfloat16),
        in_specs=[hbm] * 4 + [vmem] * 7,
        out_specs=vmem,
        scratch_shapes=[
            pltpu.VMEM((N_X, rows, cut), jnp.bfloat16),
            pltpu.VMEM((rows, D), jnp.bfloat16),
            pltpu.VMEM((rows, D), jnp.bfloat16),
            pltpu.VMEM((rows, wide), jnp.float32),
            pltpu.VMEM((rows, wide), jnp.float32),
            pltpu.VMEM((rows, HD), jnp.float32),
            pltpu.VMEM((heads, rows, HD), jnp.bfloat16),
            pltpu.VMEM((3 * N_Y * N_CORE, 2, rows, HD), jnp.bfloat16),
            pltpu.VMEM((heads, rows, 2 * HD), jnp.float32),
            pltpu.VMEM((2 * D, heads * HD), jnp.bfloat16),
            pltpu.VMEM((2 * D, w_kv.shape[1]), jnp.bfloat16),
            dma((8,)), dma((8,)), dma((4,)), dma((4,)), dma((18,)), dma((18,)), dma((24,)), dma((24,)),
            dma((4,)),
        ],
        compiler_params=pltpu.CompilerParams(
            collective_id=3, has_side_effects=True, vmem_limit_bytes=56 << 20
        ),
        name="draft",
    )(
        merged, embed, w_query, w_kv, embed_gain[None, :], merged_gain[None, :], q_gain[None, :],
        k_gain[None, :], cosine, sine, row_start,
    )


def body(
    tokens,
    low_tap,
    mid_tap,
    next_embed,
    expert_ids,
    gate_weights,
    segments,
    moe_gain,
    w_gate,
    w_up,
    w_down,
    merge_weight,
    embed_gain,
    merged_gain,
    w_query,
    w_kv,
    q_gain,
    k_gain,
):
    half = HD // 2
    freqs = np.power(THETA, -np.arange(half) * 2.0 / HD).astype(np.float32)
    freqs = np.concatenate([freqs, freqs])[None, :]
    merged, embed_rows, cosine, sine, row_start = experts(
        tokens, expert_ids.T, gate_weights.T, low_tap, mid_tap, next_embed, w_gate[0], w_up[0],
        w_down[0], merge_weight, moe_gain[None, :], segments.reshape(-1, HD), jnp.asarray(freqs),
    )
    return draft(
        merged, embed_rows, w_query, w_kv.reshape(w_kv.shape[0], -1), embed_gain, merged_gain,
        q_gain, k_gain, cosine, sine, row_start,
    )


def solution(mesh):
    return jax.shard_map(
        body,
        mesh=mesh,
        in_specs=(
            P(("expert", "group"), None),
            P(("expert", "group"), None),
            P(("expert", "group"), None),
            P(("expert", "group"), None),
            P(("expert", "group"), None),
            P(("expert", "group"), None),
            P(),
            P(),
            P(("expert", "group"), None, None),
            P(("expert", "group"), None, None),
            P(("expert", "group"), None, None),
            P(None, "group"),
            P(),
            P(),
            P(None, "group"),
            P(None, None, "group"),
            P(),
            P(),
        ),
        out_specs=P("expert", "group"),
        check_vma=False,
    )
```

```python
import jax
import jax.numpy as jnp
import numpy as np
from jax import lax
from jax.experimental import pallas as pl
from jax.experimental.pallas import tpu as pltpu
from jax.sharding import PartitionSpec as P

D = 2048
HD = 128
TOPK = 8
SEGS = 4


EPSILON = 1e-06
THETA = 1000000.0
LOG2E = 1.4426950408889634
MESH = pl.DeviceIdType.MESH
N_Z, N_Y, N_CORE, N_X = 4, 4, 2, 4
PEERS = N_Z * N_Y * N_CORE
ROUND = 8
WINDOW = 16
CUTS = 4
HALVES = (0, 1)
CAPACITY = 12
NOWHERE = -1000.0


def offset_of(slot):
    turn = slot // N_CORE
    return ((turn // N_Y + turn) % N_Z, turn % N_Y, slot % N_CORE)


def peer(offset, sign=1):
    here = lax.axis_index("expert")
    z = (here // (N_Y * N_CORE) + sign * offset[0] + N_Z) % N_Z
    y = (here // N_CORE % N_Y + sign * offset[1] + N_Y) % N_Y
    core = (here + offset[2]) % N_CORE
    return (z * N_Y + y) * N_CORE + core


def remote(source, target, sends, arrivals, slot, device):
    return pltpu.make_async_remote_copy(
        src_ref=source,
        dst_ref=target,
        send_sem=sends.at[slot],
        recv_sem=arrivals.at[slot],
        device_id=device,
        device_id_type=MESH,
    )


def greet(devices):
    barrier = pltpu.get_barrier_semaphore()
    for device in devices:
        pl.semaphore_signal(barrier, inc=1, device_id=device, device_id_type=MESH)
    pl.semaphore_wait(barrier, len(devices))


def across(step):
    return (lax.axis_index("expert"), (lax.axis_index("group") + step) % N_X)


def experts_kernel(
    tokens, choices, gates, low, mid, embed, w_gate, w_up, w_down, w_merge, gain, segments, freqs,
    merged, embed_rows, cosine, sine, row_start,
    routing, route, place, weights, shares, all_tokens, packed, arrived, normed, hidden, returned,
    total, partial, halves, high, low_rows, mid_rows, merge_total,
    gate_mat, up_mat, down_mat, merge_mat,
    own, route_sends, route_arrivals, token_sends, token_arrivals, out_sends, out_arrivals,
    back_sends, back_arrivals, tap_sends, tap_arrivals, sum_sends, sum_arrivals,
    high_sends, high_arrivals,
):
    x = lax.axis_index("group")
    rows = tokens.shape[0]
    slots = CAPACITY * N_X
    batch = ROUND * slots
    batches = PEERS // ROUND
    cut = D // CUTS
    steps = range(1, N_X)
    mine = pl.ds(pl.multiple_of(x * rows, rows), rows)

    def columns(part):
        return pl.ds(pl.multiple_of(part * cut, cut), cut)

    def slot_rows(slot):
        return pl.ds(pl.multiple_of(slot * slots, slots), slots)

    def batch_rows(index):
        return pl.ds(pl.multiple_of(index * batch, batch), batch)

    kept = [
        pltpu.make_async_copy(source, target, own.at[index])
        for index, (source, target) in enumerate(
            (
                (tokens, all_tokens.at[mine]),
                (w_gate, gate_mat),
                (w_up, up_mat),
                (w_down, down_mat),
                (low, low_rows.at[mine]),
                (mid, mid_rows.at[mine]),
                (w_merge, merge_mat),
                (embed, embed_rows.at[mine]),
            )
        )
    ]
    for copy in kept:
        copy.start()

    barrier = pltpu.get_barrier_semaphore()
    for step in steps:
        pl.semaphore_signal(barrier, inc=1, device_id=across(step), device_id_type=MESH)

    @pl.loop(1, PEERS)
    def _(slot):
        pl.semaphore_signal(
            barrier, inc=1, device_id=(peer(offset_of(slot), -1), x), device_id_type=MESH
        )

    slot = lax.broadcasted_iota(jnp.int32, (PEERS, 1), 0)
    owner = peer(offset_of(slot)) * N_X
    earlier = lax.broadcasted_iota(jnp.int32, (rows, rows), 0) < lax.broadcasted_iota(
        jnp.int32, (rows, rows), 1
    )
    earlier = jnp.where(earlier, 1.0, 0.0).astype(jnp.bfloat16)
    for plane in range(N_X):
        member = jnp.zeros((PEERS, rows), jnp.float32)
        share = jnp.zeros((PEERS, rows), jnp.float32)
        for choice in range(TOPK):
            hit = choices[choice : choice + 1, :] == owner + plane
            member += jnp.where(hit, 1.0, 0.0)
            share += jnp.where(hit, gates[choice : choice + 1, :], 0.0)
        ranks = jnp.dot(member.astype(jnp.bfloat16), earlier, preferred_element_type=jnp.float32)
        shift = (CAPACITY * x).astype(jnp.float32)
        routing[plane, 0] = jnp.where(member > 0.0, ranks + shift, NOWHERE)
        routing[plane, 1] = share

    pl.semaphore_wait(barrier, PEERS - 1 + N_X - 1)

    def route_copy(step):
        return remote(
            routing.at[(x + step) % N_X], route.at[x], route_sends, route_arrivals, step - 1,
            across(step),
        )

    def token_copy(part, step):
        return remote(
            tokens.at[:, columns(part)], all_tokens.at[mine, columns(part)],
            token_sends, token_arrivals, (N_X - 1) * part + step - 1, across(step),
        )

    def outward(slot, part):
        return remote(
            packed.at[slot_rows(slot), columns(part)], arrived.at[slot_rows(slot), columns(part)],
            out_sends, out_arrivals, PEERS * part + slot, (peer(offset_of(slot)), x),
        )

    def homeward(slot, part):
        return remote(
            packed.at[slot_rows(slot), columns(part)], returned.at[slot_rows(slot), columns(part)],
            back_sends, back_arrivals, PEERS * part + slot, (peer(offset_of(slot), -1), x),
        )

    def tap_copy(index, step):
        source = (low, mid, embed)[index]
        target = (low_rows, mid_rows, embed_rows)[index]
        return remote(
            source, target.at[mine], tap_sends, tap_arrivals, (N_X - 1) * index + step - 1,
            across(step),
        )

    def sum_copy(part, step):
        theirs = pl.ds(pl.multiple_of((x + step) % N_X * rows, rows), rows)
        return remote(
            partial.at[theirs, columns(part)], halves.at[step - 1, :, columns(part)],
            sum_sends, sum_arrivals, (N_X - 1) * part + step - 1, across(step),
        )

    def high_copy(part, step):
        return remote(
            high.at[mine, columns(part)], high.at[mine, columns(part)],
            high_sends, high_arrivals, (N_X - 1) * part + step - 1, across(step),
        )

    for step in steps:
        route_copy(step).start()
    for part in range(2):
        for step in steps:
            token_copy(part, step).start()
    route[x] = routing[x]
    for step in steps:
        route_copy(step).wait_recv()

    def spread_line(kind, slot):
        return jnp.concatenate(
            [route[block, kind, pl.ds(slot, 1), :] for block in range(N_X)], axis=1
        )

    def match(slot):
        lines = lax.broadcasted_iota(jnp.int32, (slots, N_X * rows), 0).astype(jnp.float32)
        return lines == spread_line(0, slot)

    @pl.loop(0, PEERS)
    def _(slot):
        place[slot_rows(slot), :] = jnp.where(match(slot), 1.0, 0.0).astype(jnp.bfloat16)

    kept[0].wait()

    @pl.loop(0, CUTS)
    def _(part):
        for step in steps:
            token_copy(part, step).wait_recv()

        @pl.when(part + 2 < CUTS)
        def _():
            for step in steps:
                token_copy(part + 2, step).start()

        @pl.loop(0, batches)
        def _(index):
            span = batch_rows(index)
            packed[span, columns(part)] = jnp.dot(
                place[span, :], all_tokens[:, columns(part)], preferred_element_type=jnp.float32
            ).astype(jnp.bfloat16)

            @pl.loop(index * ROUND, (index + 1) * ROUND)
            def _(slot):
                pl.when(slot > 0)(lambda: outward(slot, part).start())

        arrived[slot_rows(0), columns(part)] = packed[slot_rows(0), columns(part)]

    for index in range(3):
        for step in steps:
            tap_copy(index, step).start()

    @pl.loop(0, batches)
    def _(index):
        @pl.loop(0, ROUND)
        def _(inner):
            slot = index * ROUND + inner
            weights[slot_rows(inner), :] = jnp.where(match(slot), spread_line(1, slot), 0.0)

        shares[:, batch_rows(index)] = weights[...].T.astype(jnp.bfloat16)

    line = lax.axis_index("expert") * N_X * rows + lax.broadcasted_iota(
        jnp.int32, (N_X * rows, 1), 0
    )
    line = line.astype(jnp.float32)
    start = jnp.zeros_like(line)
    for label in range(1, SEGS):
        below = jnp.where(segments[...] < label, 1.0, 0.0)
        count = jnp.sum(jnp.sum(below, axis=1, keepdims=True), axis=0, keepdims=True)
        start = jnp.maximum(start, jnp.where(count <= line, count, 0.0))
    row_start[...] = start.astype(jnp.int32)
    angles = (line - start) * freqs[...]
    signs = jnp.where(lax.broadcasted_iota(jnp.int32, (1, HD), 1) < HD // 2, -1.0, 1.0)
    cosine[...] = jnp.cos(angles)
    sine[...] = jnp.sin(angles) * signs
    for copy in kept[1:]:
        copy.wait()

    def reply(index, part):
        span = batch_rows(index)
        packed[span, columns(part)] = jnp.dot(
            hidden[span, :], down_mat[:, columns(part)], preferred_element_type=jnp.float32
        ).astype(jnp.bfloat16)

        @pl.loop(index * ROUND, (index + 1) * ROUND)
        def _(slot):
            pl.when(slot > 0)(lambda: homeward(slot, part).start())

        @pl.when(index == 0)
        def _():
            returned[slot_rows(0), columns(part)] = packed[slot_rows(0), columns(part)]

    def each_copy(index, act):
        @pl.loop(0, ROUND * CUTS)
        def _(inner):
            slot = index * ROUND + inner % ROUND
            pl.when(slot > 0)(lambda: act(slot, inner // ROUND))

    @pl.loop(0, batches)
    def _(index):
        each_copy(index, lambda slot, part: outward(slot, part).wait_recv())

        @pl.loop(0, ROUND)
        def _(inner):
            values = arrived[slot_rows(index * ROUND + inner), :].astype(jnp.float32)
            size = lax.rsqrt(jnp.mean(values * values, axis=-1, keepdims=True) + EPSILON)
            normed[slot_rows(inner), :] = (values * size * gain[...]).astype(jnp.bfloat16)

        @pl.loop(0, w_gate.shape[1] // 256)
        def _(tile):
            tiles = pl.ds(pl.multiple_of(tile * 256, 256), 256)
            gate = jnp.dot(normed[...], gate_mat[:, tiles], preferred_element_type=jnp.float32)
            up = jnp.dot(normed[...], up_mat[:, tiles], preferred_element_type=jnp.float32)
            hidden[batch_rows(index), tiles] = (gate / (1.0 + jnp.exp(-gate)) * up).astype(
                jnp.bfloat16
            )

        each_copy(index, lambda slot, part: outward(slot, part).wait_send())
        reply(index, 0)

    @pl.loop(batches, CUTS * batches)
    def _(turn):
        reply(turn % batches, turn // batches)

    for index in range(2):
        for step in steps:
            tap_copy(index, step).wait_recv()
    merge_total[...] = jnp.zeros_like(merge_total)

    def add_merge(source, index, part):
        depth = pl.ds(pl.multiple_of(index * D + part * cut, cut), cut)
        merge_total[...] += jnp.dot(
            source[:, columns(part)], merge_mat[depth, :], preferred_element_type=jnp.float32
        )

    @pl.loop(0, CUTS)
    def _(part):
        add_merge(low_rows, 0, part)
        add_merge(mid_rows, 1, part)

    def add_high(part):
        for step in steps:
            high_copy(part, step).wait_recv()
        add_merge(high, 2, part)

    @pl.loop(0, CUTS)
    def _(part):
        total[...] = jnp.zeros_like(total)

        @pl.loop(0, batches)
        def _(index):
            @pl.loop(index * ROUND, (index + 1) * ROUND)
            def _(slot):
                pl.when(slot > 0)(lambda: homeward(slot, part).wait_recv())

            span = batch_rows(index)
            total[...] += jnp.dot(
                shares[:, span], returned[span, columns(part)], preferred_element_type=jnp.float32
            )

        partial[:, columns(part)] = total[...].astype(jnp.bfloat16)
        for step in steps:
            sum_copy(part, step).start()
        mixed = all_tokens[mine, columns(part)].astype(jnp.float32) + total[mine, :]
        for step in steps:
            sum_copy(part, step).wait_recv()
            mixed += halves[step - 1, :, columns(part)].astype(jnp.float32)
        high[mine, columns(part)] = mixed.astype(jnp.bfloat16)
        for step in steps:
            high_copy(part, step).start()
        pl.when(part > 0)(lambda: add_high(part - 1))

    add_high(CUTS - 1)
    merged[...] = merge_total[...].astype(jnp.bfloat16)

    @pl.loop(0, batches)
    def _(index):
        each_copy(index, lambda slot, part: homeward(slot, part).wait_send())

    for step in steps:
        route_copy(step).wait_send()
        tap_copy(2, step).wait_recv()
        for index in range(3):
            tap_copy(index, step).wait_send()

        @pl.loop(0, CUTS)
        def _(part):
            token_copy(part, step).wait_send()
            sum_copy(part, step).wait_send()
            high_copy(part, step).wait_send()


def experts(
    tokens, choices, gates, low, mid, embed, w_gate, w_up, w_down, w_merge, gain, segments, freqs
):
    rows, width, out_width = tokens.shape[0], w_gate.shape[1], w_merge.shape[1]
    everyone = N_X * rows
    slots = CAPACITY * N_X
    hbm = pl.BlockSpec(memory_space=pl.ANY)
    vmem = pl.BlockSpec(memory_space=pltpu.VMEM)
    dma = pltpu.SemaphoreType.DMA

    def half(*shape):
        return pltpu.VMEM(shape, jnp.bfloat16)

    def full(*shape):
        return pltpu.VMEM(shape, jnp.float32)

    few, many = (N_X - 1) * CUTS, PEERS * CUTS
    return pl.pallas_call(
        experts_kernel,
        out_shape=(
            jax.ShapeDtypeStruct((everyone, out_width), jnp.bfloat16),
            jax.ShapeDtypeStruct((everyone, D), jnp.bfloat16),
            jax.ShapeDtypeStruct((everyone, HD), jnp.float32),
            jax.ShapeDtypeStruct((everyone, HD), jnp.float32),
            jax.ShapeDtypeStruct((everyone, 1), jnp.int32),
        ),
        in_specs=[hbm, vmem, vmem] + [hbm] * 7 + [vmem] * 3,
        out_specs=(vmem, hbm, vmem, vmem, vmem),
        scratch_shapes=[
            full(N_X, 2, PEERS, rows),
            full(N_X, 2, PEERS, rows),
            half(PEERS * slots, everyone),
            full(ROUND * slots, everyone),
            half(everyone, PEERS * slots),
            half(everyone, D),
            half(PEERS * slots, D),
            half(PEERS * slots, D),
            half(ROUND * slots, D),
            half(PEERS * slots, width),
            half(PEERS * slots, D),
            full(everyone, D // CUTS),
            half(everyone, D),
            half(N_X - 1, rows, D),
            half(everyone, D),
            half(everyone, D),
            half(everyone, D),
            full(everyone, out_width),
            half(D, width),
            half(D, width),
            half(width, D),
            half(3 * D, out_width),
            dma((9,)),
            dma((N_X - 1,)), dma((N_X - 1,)),
            dma((few,)), dma((few,)),
            dma((many,)), dma((many,)),
            dma((many,)), dma((many,)),
            dma((9,)), dma((9,)),
            dma((few,)), dma((few,)),
            dma((few,)), dma((few,)),
        ],
        compiler_params=pltpu.CompilerParams(
            collective_id=2, has_side_effects=True, vmem_limit_bytes=60 << 20
        ),
        cost_estimate=pl.CostEstimate(
            flops=6 * PEERS * slots * D * width, bytes_accessed=40 << 20, transcendentals=0
        ),
        name="experts",
    )(
        tokens, choices, gates, low, mid, embed, w_gate, w_up, w_down, w_merge, gain, segments, freqs
    )


def draft_kernel(
    merged, embed, w_query, w_kv, embed_gain, merged_gain, q_gain, k_gain, cosine, sine, row_start,
    out,
    pieces, embeds, joined, embed_total, merged_total, squares, query, held, total,
    query_mat, kv_mat,
    x_sends, x_arrivals, z_sends, z_arrivals, y_sends, y_arrivals, core_sends, core_arrivals, own,
):
    rows, cut = merged.shape
    heads = query.shape[0]
    here, x = lax.axis_index("expert"), lax.axis_index("group")
    z, y, core = here // (N_Y * N_CORE), here // N_CORE % N_Y, here % N_CORE
    loads = [
        pltpu.make_async_copy(source, target, own.at[index])
        for index, (source, target) in enumerate(
            ((merged, pieces.at[x]), (embed, embeds), (w_query, query_mat), (w_kv, kv_mat))
        )
    ]
    for load in loads:
        load.start()
    greet(
        [across(step) for step in (1, 2, 3)]
        + [(peer((step, 0, 0)), x) for step in (1, 2, 3)]
        + [(peer((0, step, 0)), x) for step in (1, 2, 3)]
        + [(peer((0, 0, 1)), x)]
    )
    near, far = 1, N_X - 1
    size = rows // len(HALVES)

    def span_of(half):
        return pl.ds(half * size, size)

    def direct(index, half):
        span = span_of(half)
        return remote(
            merged.at[span], pieces.at[x, span], x_sends, x_arrivals, 4 * half + index,
            across((near, far)[index]),
        )

    def onward(index, half):
        block = (x + (far, near)[index]) % N_X
        span = pl.ds(half * size + index * size // 2, size // 2)
        return remote(
            pieces.at[block, span], pieces.at[block, span], x_sends, x_arrivals,
            4 * half + 2 + index, across((near, far)[index]),
        )

    for index in (0, 1):
        direct(index, 0).start()

    def add_part(source, depth, target):
        target[:, : heads * HD] += jnp.dot(
            source, query_mat[depth, :], preferred_element_type=jnp.float32
        )
        target[:, heads * HD :] += jnp.dot(
            source, kv_mat[depth, :], preferred_element_type=jnp.float32
        )

    def columns(part):
        return pl.ds(pl.multiple_of(part * cut, cut), cut)

    embed_total[...] = jnp.zeros_like(embed_total)
    merged_total[...] = jnp.zeros_like(merged_total)
    squares[...] = jnp.zeros_like(squares)
    loads[1].wait()
    chunk = rows // 8

    @pl.loop(0, 8)
    def _(index):
        span = pl.ds(pl.multiple_of(index * chunk, chunk), chunk)
        values = embeds[span, :].astype(jnp.float32)
        size = lax.rsqrt(jnp.mean(values * values, axis=-1, keepdims=True) + EPSILON)
        joined[span, :] = (values * size * embed_gain[...]).astype(jnp.bfloat16)

    for index in (0, 1):
        direct(index, 0).wait_recv()
        onward(index, 0).start()
        direct(index, 1).start()
    for load in (loads[0], loads[2], loads[3]):
        load.wait()

    @pl.loop(0, N_X)
    def _(part):
        add_part(joined[:, columns(part)], columns(part), embed_total)

    def add_piece(block, half):
        span = span_of(half)
        values = pieces[block, span].astype(jnp.float32)
        squares[span, :] += jnp.broadcast_to(
            jnp.sum(values * values, axis=-1, keepdims=True), (size, HD)
        )
        source = (values * merged_gain[:, columns(block)]).astype(jnp.bfloat16)
        joined[span, columns(block)] = source
        depth = pl.ds(pl.multiple_of(D + block * cut, cut), cut)
        merged_total[span, heads * HD :] += jnp.dot(
            source, kv_mat[depth, :], preferred_element_type=jnp.float32
        )

    def project(index, span):
        shrink = lax.rsqrt(squares[span, :1] * (1.0 / D) + EPSILON)
        lanes = slice(index * HD, (index + 1) * HD)
        return embed_total[span, lanes] + merged_total[span, lanes] * shrink

    def turned(values, gain, span):
        scale = lax.rsqrt(jnp.mean(values * values, axis=-1, keepdims=True) + EPSILON)
        values = values * scale * gain[...]
        return values * cosine[span, :] + pltpu.roll(values, HD // 2, 1) * sine[span, :]

    def place(plane, row, column):
        return (plane * N_Y + row) * N_CORE + column

    def wanted(plane, row, reader):
        near = (plane == 0) & (row <= reader)
        return near | ((plane == 1) & (z >= 1)) | ((plane == 2) & (z >= 2) & (row >= reader))

    def along_z(plane, half):
        span = span_of(half)
        return remote(
            held.at[place(0, y, core), :, span], held.at[place(plane, y, core), :, span],
            z_sends, z_arrivals, 2 * (plane - 1) + half, (peer((plane, 0, 0)), x),
        )

    def along_y(plane, step, half):
        part = held.at[place(plane, y, core), :, span_of(half)]
        return remote(
            part, part, y_sends, y_arrivals, 2 * (3 * plane + step - 1) + half,
            (peer((0, step, 0)), x),
        )

    def from_y(plane, step, row, half):
        part = held.at[place(plane, row, core), :, span_of(half)]
        return remote(
            part, part, y_sends, y_arrivals, 2 * (3 * plane + step - 1) + half,
            (peer((0, 1, 0)), x),
        )

    def sibling(plane, row, column, half):
        part = held.at[place(plane, row, column), :, span_of(half)]
        return remote(
            part, part, core_sends, core_arrivals, 2 * (N_Y * plane + row) + half,
            (peer((0, 0, 1)), x),
        )

    def share(plane, half):
        for step in (1, 2, 3):
            pl.when(wanted(plane, y, (y + step) % N_Y))(along_y(plane, step, half).start)

    total[...] = jnp.zeros_like(total)
    for half in HALVES:
        for turn in (0, 3, 1):
            add_piece((x + turn) % N_X, half)
        if half == 0:
            for index in (0, 1):
                direct(index, 1).wait_recv()
                onward(index, 1).start()
        for index in (0, 1):
            onward(index, half).wait_recv()
        add_piece((x + 2) % N_X, half)
        span = span_of(half)
        mine = place(0, y, core)
        held[mine, 0, span] = turned(project(heads, span), k_gain, span).astype(jnp.bfloat16)
        held[mine, 1, span] = project(heads + 1, span).astype(jnp.bfloat16)
        for plane in (2, 1):
            pl.when(z + plane < N_Z)(along_z(plane, half).start)
        share(0, half)
        sibling(0, y, core, half).start()

    def pass_plane(plane, half):
        @pl.when(z >= plane)
        def _():
            along_z(plane, half).wait_recv()
            share(plane, half)
            pl.when(wanted(plane, y, y))(sibling(plane, y, core, half).start)

    pass_plane(1, 0)

    @pl.loop(0, N_X)
    def _(part):
        depth = pl.ds(pl.multiple_of(D + part * cut, cut), cut)
        merged_total[:, : heads * HD] += jnp.dot(
            joined[:, columns(part)], query_mat[depth, :], preferred_element_type=jnp.float32
        )

    everything = pl.ds(0, rows)
    for index in range(heads):
        query[index] = (
            turned(project(index, everything), q_gain, everything) * (HD**-0.5 * LOG2E)
        ).astype(jnp.bfloat16)

    def add_block(plane, row, column):
        slot = place(plane, row, column)
        first = ((z - plane) * N_Y * N_CORE + row * N_CORE + column) * rows
        key = held[slot, 0]
        value = jnp.concatenate([held[slot, 1], jnp.ones((rows, HD), jnp.bfloat16)], axis=1)
        query_index = here * rows + lax.broadcasted_iota(jnp.int32, (rows, rows), 0)
        key_index = first + lax.broadcasted_iota(jnp.int32, (rows, rows), 1)
        allowed = (key_index <= query_index) & (key_index >= row_start[...])
        for head in range(heads):
            scores = lax.dot_general(
                query[head], key, (((1,), (1,)), ((), ())), preferred_element_type=jnp.float32
            )
            weights = jnp.where(allowed, jnp.exp2(scores), 0.0).astype(jnp.bfloat16)
            total[head] += jnp.dot(weights, value, preferred_element_type=jnp.float32)

    def needed(plane, row, column):
        behind = here - ((z - plane) * N_Y * N_CORE + row * N_CORE + column)
        return wanted(plane, row, y) & (behind >= 0) & (behind <= WINDOW)

    pass_plane(1, 1)
    add_block(0, y, core)
    @pl.loop(1, 3 * N_Y + 1)
    def _(step):
        @pl.when(step == jnp.where(y == 0, 2 * N_Y, N_Y - 1))
        def _():
            for half in HALVES:
                pass_plane(2, half)

        plane, back = step // N_Y, step % N_Y
        row = (y + N_Y - back) % N_Y

        @pl.when((step < 3 * N_Y) & wanted(plane, row, y))
        def _():
            @pl.when(back > 0)
            def _():
                for half in HALVES:
                    from_y(plane, back, row, half).wait_recv()
                    sibling(plane, row, core, half).start()

            pl.when(needed(plane, row, core))(lambda: add_block(plane, row, core))

        plane, back = (step - 1) // N_Y, (step - 1) % N_Y
        row = (y + N_Y - back) % N_Y

        @pl.when(wanted(plane, row, y))
        def _():
            for half in HALVES:
                sibling(plane, row, 1 - core, half).wait_recv()
            pl.when(needed(plane, row, 1 - core))(lambda: add_block(plane, row, 1 - core))

    for head in range(heads):
        out[:, head * HD : (head + 1) * HD] = (
            total[head, :, :HD] / total[head, :, HD:]
        ).astype(out.dtype)
    for half in HALVES:
        for plane in (1, 2):
            pl.when(z + plane < N_Z)(along_z(plane, half).wait_send)
        for plane in (0, 1, 2):
            for step in (1, 2, 3):
                pl.when(wanted(plane, y, (y + step) % N_Y))(along_y(plane, step, half).wait_send)
            for row in range(N_Y):
                pl.when(wanted(plane, row, y))(sibling(plane, row, core, half).wait_send)
        for index in (0, 1):
            direct(index, half).wait_send()
            onward(index, half).wait_send()


def draft(merged, embed, w_query, w_kv, embed_gain, merged_gain, q_gain, k_gain, cosine, sine, row_start):
    rows, cut = merged.shape
    heads = w_query.shape[1] // HD
    wide = w_query.shape[1] + w_kv.shape[1]
    hbm = pl.BlockSpec(memory_space=pl.ANY)
    vmem = pl.BlockSpec(memory_space=pltpu.VMEM)
    dma = pltpu.SemaphoreType.DMA
    return pl.pallas_call(
        draft_kernel,
        out_shape=jax.ShapeDtypeStruct((rows, heads * HD), jnp.bfloat16),
        in_specs=[hbm] * 4 + [vmem] * 7,
        out_specs=vmem,
        scratch_shapes=[
            pltpu.VMEM((N_X, rows, cut), jnp.bfloat16),
            pltpu.VMEM((rows, D), jnp.bfloat16),
            pltpu.VMEM((rows, D), jnp.bfloat16),
            pltpu.VMEM((rows, wide), jnp.float32),
            pltpu.VMEM((rows, wide), jnp.float32),
            pltpu.VMEM((rows, HD), jnp.float32),
            pltpu.VMEM((heads, rows, HD), jnp.bfloat16),
            pltpu.VMEM((3 * N_Y * N_CORE, 2, rows, HD), jnp.bfloat16),
            pltpu.VMEM((heads, rows, 2 * HD), jnp.float32),
            pltpu.VMEM((2 * D, heads * HD), jnp.bfloat16),
            pltpu.VMEM((2 * D, w_kv.shape[1]), jnp.bfloat16),
            dma((8,)), dma((8,)), dma((4,)), dma((4,)), dma((18,)), dma((18,)), dma((24,)), dma((24,)),
            dma((4,)),
        ],
        compiler_params=pltpu.CompilerParams(
            collective_id=3, has_side_effects=True, vmem_limit_bytes=56 << 20
        ),
        name="draft",
    )(
        merged, embed, w_query, w_kv, embed_gain[None, :], merged_gain[None, :], q_gain[None, :],
        k_gain[None, :], cosine, sine, row_start,
    )


def body(
    tokens,
    low_tap,
    mid_tap,
    next_embed,
    expert_ids,
    gate_weights,
    segments,
    moe_gain,
    w_gate,
    w_up,
    w_down,
    merge_weight,
    embed_gain,
    merged_gain,
    w_query,
    w_kv,
    q_gain,
    k_gain,
):
    half = HD // 2
    freqs = np.power(THETA, -np.arange(half) * 2.0 / HD).astype(np.float32)
    freqs = np.concatenate([freqs, freqs])[None, :]
    merged, embed_rows, cosine, sine, row_start = experts(
        tokens, expert_ids.T, gate_weights.T, low_tap, mid_tap, next_embed, w_gate[0], w_up[0],
        w_down[0], merge_weight, moe_gain[None, :], segments.reshape(-1, HD), jnp.asarray(freqs),
    )
    return draft(
        merged, embed_rows, w_query, w_kv.reshape(w_kv.shape[0], -1), embed_gain, merged_gain,
        q_gain, k_gain, cosine, sine, row_start,
    )


def solution(mesh):
    return jax.shard_map(
        body,
        mesh=mesh,
        in_specs=(
            P(("expert", "group"), None),
            P(("expert", "group"), None),
            P(("expert", "group"), None),
            P(("expert", "group"), None),
            P(("expert", "group"), None),
            P(("expert", "group"), None),
            P(),
            P(),
            P(("expert", "group"), None, None),
            P(("expert", "group"), None, None),
            P(("expert", "group"), None, None),
            P(None, "group"),
            P(),
            P(),
            P(None, "group"),
            P(None, None, "group"),
            P(),
            P(),
        ),
        out_specs=P("expert", "group"),
        check_vma=False,
    )
```
